128 devices in a mesh: blk: 32 (over x_lo, y, z), corpus: 4 (over x_hi, core).
Axes of the slice: x: 4 (x_hi: 2, x_lo: 2; x = x_hi * 2 + x_lo), y: 4, z: 4, core: 2. Of those that a mesh axis runs over, the one named last changes fastest.
Arguments:
- queries: bfloat16 [4096, 4096], P('blk', 'corpus'), may hold values from -12 to 12
- passages: bfloat16 [4096, 4096], P('blk', 'corpus'), may hold values from -4 to 4
- table: bfloat16 [1024, 4096], P('corpus'), may hold values from -4 to 4
- neg_owner: int32 [4096, 7], P('blk'), may hold values from 0 to 3, as said below
- neg_row: int32 [4096, 7], P('blk'), may hold values from 0 to 255
- positive: int32 [4096], P('blk'), may hold values from 0 to 4095, each once
- loss_weight: float32 [4096], P('blk'), may hold values from 32 to 256
Outputs:
- losses: float32 [4096], P(('blk', 'corpus'))
- query_grad: float32 [4096, 4096], P('blk', 'corpus')
- passage_grad: float32 [4096, 4096], P('blk', 'corpus')
- table_grad: float32 [1024, 4096], P('corpus', 'blk')
The draws below stay inside these ranges and needn't reach their ends.
Inputs may be any that keep to these rules, and one draw needn't show every extreme that they name: `neg_owner`: among the 896 references of the queries of one index of blk (aligned blocks of 128 queries), one shard is named exactly 448 times and no shard more often.
All inputs are finite; a program needn't handle non-finite values.
Results may differ from the reference program's by a relative error of at most 0.0065.
Values may be sent and summed in bfloat16 or wider, within the bound.
A program may use at most 128 MiB of HBM per device.

```python
import math
import jax
import jax.numpy as jnp

D = 4096
Q_BLK = 128
NEGS = 7
ROWS_SH = 256
B = 4096
CAP = 448
CROWS = 1024
N_CORPUS = 4


def common_draw(key):
    block_refs = Q_BLK * NEGS
    blocks = B // Q_BLK
    hot_owner = jax.random.randint(jax.random.fold_in(key, 11), (blocks, 1), 0, N_CORPUS)
    offsets = jax.random.randint(jax.random.fold_in(key, 12), (blocks, block_refs), 1, N_CORPUS)
    places = jnp.arange(block_refs)[None, :]
    ordered = jnp.where(places < CAP, hot_owner, (hot_owner + offsets) % N_CORPUS)
    block_keys = jax.random.split(jax.random.fold_in(key, 13), blocks)
    orders = jax.vmap(lambda sub_key: jax.random.permutation(sub_key, block_refs))(block_keys)
    owners = jnp.take_along_axis(ordered, orders, axis=1).reshape(B, NEGS).astype(jnp.int32)
    shard_rows = jax.random.randint(jax.random.fold_in(key, 14), (B, NEGS), 0, ROWS_SH).astype(jnp.int32)
    table = jnp.clip(jax.random.normal(jax.random.fold_in(key, 15), (CROWS, D)), -4.0, 4.0)
    passages = jnp.clip(jax.random.normal(jax.random.fold_in(key, 16), (B, D)), -4.0, 4.0)
    noise = jnp.clip(jax.random.normal(jax.random.fold_in(key, 18), (B, D)), -4.0, 4.0)
    table_ids = owners * ROWS_SH + shard_rows
    hard_sum = jnp.zeros((B, D), jnp.float32)
    for which in range(NEGS):
        hard_sum = hard_sum + table[table_ids[:, which]]
    queries = noise + 0.07 * hard_sum
    return (owners, shard_rows, table, passages, queries)


def draw_queries(key, part):
    return common_draw(key)[4].astype(jnp.bfloat16)


def draw_passages(key, part):
    return common_draw(key)[3].astype(jnp.bfloat16)


def draw_table(key, part):
    return common_draw(key)[2].astype(jnp.bfloat16)


def draw_neg_owner(key, part):
    return common_draw(key)[0]


def draw_neg_row(key, part):
    return common_draw(key)[1]


def shard_levels(stream_key, dims, cuts, least, largest):
    gain, own = 1.0, jax.random.fold_in(stream_key, 6)
    for dim, parts in cuts:
        steps = jnp.exp(jax.random.uniform(jax.random.fold_in(own, dim), (parts,), jnp.float32, least / len(cuts), largest / len(cuts)))
        gain = gain * jnp.repeat(steps, dims[dim] // parts).reshape([-1 if axis == dim else 1 for axis in range(len(dims))])
    return gain


def setup_inputs(seed: int = 0) -> dict:
    keys = jax.random.split(jax.random.key(seed), 8)
    queries = draw_queries(jax.random.fold_in(keys[7], 71), 0)
    passages = draw_passages(jax.random.fold_in(keys[7], 71), 0)
    table = draw_table(jax.random.fold_in(keys[7], 71), 0)
    neg_owner = draw_neg_owner(jax.random.fold_in(keys[7], 71), 0)
    neg_row = draw_neg_row(jax.random.fold_in(keys[7], 71), 0)
    positive = jax.random.permutation(keys[5], B).astype(jnp.int32)
    loss_weight = jnp.clip(jnp.exp(math.log(256.0) - 2.0794415 * jax.random.uniform(keys[6], (B,), jnp.float32) ** shard_levels(keys[6], (B,), ((0, 32),), -0.2, 0.2)), 32.0, 256.0)
    return {"queries": queries, "passages": passages, "table": table, "neg_owner": neg_owner, "neg_row": neg_row, "positive": positive, "loss_weight": loss_weight}


def reference(queries, passages, table, neg_owner, neg_row, positive, loss_weight):
    factor = queries.shape[1] ** -0.5
    table_ids = (neg_owner * ROWS_SH + neg_row).astype(jnp.int32)
    logits = jnp.dot(queries, passages.T, preferred_element_type=jnp.float32) * factor
    query_wide = queries.astype(jnp.float32)
    gathered = []
    hard_cols = []
    for which in range(NEGS):
        neg_rows = table[table_ids[:, which]].astype(jnp.float32)
        gathered.append(neg_rows)
        hard_cols.append(jnp.sum(query_wide * neg_rows, axis=1) * factor)
    hard_logits = jnp.stack(hard_cols, axis=1)
    row_top = jnp.maximum(jnp.max(logits, axis=1), jnp.max(hard_logits, axis=1))
    log_total = row_top + jnp.log(jnp.sum(jnp.exp(logits - row_top[:, None]), axis=1) + jnp.sum(jnp.exp(hard_logits - row_top[:, None]), axis=1))
    one_hot = positive[:, None] == jnp.arange(logits.shape[1], dtype=jnp.int32)[None, :]
    losses = log_total - jnp.sum(jnp.where(one_hot, logits, jnp.float32(0.0)), axis=1)
    weighting = (loss_weight * factor)[:, None]
    soft_grad = (weighting * (jnp.exp(logits - log_total[:, None]) - one_hot.astype(jnp.float32))).astype(jnp.bfloat16)
    hard_grad = (weighting * jnp.exp(hard_logits - log_total[:, None])).astype(jnp.bfloat16)
    query_grad = jnp.dot(soft_grad, passages, preferred_element_type=jnp.float32)
    table_grad = jnp.zeros((table.shape[0], table.shape[1]), jnp.float32)
    for which in range(NEGS):
        column_grad = hard_grad[:, which:which + 1].astype(jnp.float32)
        query_grad = query_grad + column_grad * gathered[which]
        table_grad = table_grad.at[table_ids[:, which]].add(column_grad * query_wide)
    passage_grad = jnp.dot(soft_grad.T, queries, preferred_element_type=jnp.float32)
    return losses, query_grad, passage_grad, table_grad
```

```python
import functools

import jax
import jax.numpy as jnp
from jax import lax
from jax.experimental import pallas as pl
from jax.experimental.pallas import tpu as pltpu
from jax.sharding import PartitionSpec as P

MESH = pl.DeviceIdType.MESH
F32 = jnp.float32
BF16 = jnp.bfloat16

R = 128
W = 1024
NB = 4
TR = 64
COLS = NB * R + 2 * TR
CW = 256


def device(x, y, z, k):
    return (lax.rem(x, 2) * 16 + y * 4 + z, lax.div(x, 2) * 2 + k)


def kernel(
    factor, q_in, p_in, t_in, idx_in, loss_out, qg_out, pg_out, tg_out,
    qb, pt, idx, s_own, s_far, e_buf, grad, stats, qg_part, pg_part, tg_part,
    rq, rqx, rp, rpx, rt, tt, qx, px, tsum,
    q_s, q_r, p_s, p_r, t_s, i_s, i_r, c_s, c_r, st_s, st_r,
    qg_s, qg_r, qx_s, pg_s, pg_r, px_s, px_r, tg_s, tg_r, tt_s, tt_r,
):
    b, c = lax.axis_index("blk"), lax.axis_index("corpus")
    xl, y, z = lax.div(b, 16), lax.rem(lax.div(b, 4), 4), lax.rem(b, 4)
    xh, k = lax.div(c, 2), lax.rem(c, 2)
    x = 2 * xh + xl
    far = 1 - xh
    opposite = lax.rem(x + 2, 4)
    sibling = device(x, y, z, 1 - k)

    def send(src, dst, ss, rs, where):
        copy = pltpu.make_async_remote_copy(
            src_ref=src, dst_ref=dst, send_sem=ss, recv_sem=rs, device_id=where, device_id_type=MESH
        )
        copy.start()
        return copy

    def arrive(dst, rs):
        pltpu.make_async_remote_copy(
            src_ref=dst, dst_ref=dst, send_sem=rs, recv_sem=rs, device_id=sibling, device_id_type=MESH
        ).wait_recv()

    def turn(v, d):
        return lax.rem(v + d, 4)

    barrier = pltpu.get_barrier_semaphore()
    peers = [sibling]
    for d in (1, 2, 3):
        peers.append(device(x, y, turn(z, d), k))
        peers.append(device(x, turn(y, d), z, k))
        peers.append(device(turn(x, d), y, z, k))
        peers.append(device(opposite, y, turn(z, d), k))
        peers.append(device(2 * xh + (1 - xl), turn(y, d), z, k))
    for peer in peers:
        pl.semaphore_signal(barrier, 1, device_id=peer, device_id_type=MESH)
    src_y = 2 * lax.rem(y, 2) + lax.div(z, 2)
    src_k = lax.div(y, 2)
    for zz in range(4):
        pl.semaphore_signal(barrier, 1, device_id=device(x, src_y, zz, src_k), device_id_type=MESH)
    pl.semaphore_wait(barrier, len(peers) + 4)

    def rows(i, n=R):
        return pl.ds(pl.multiple_of(i * n, n), n)

    sends = []
    for t in range(2):
        @pl.when(x != 2 * xl + t)
        def _():
            send(p_in, pt.at[xh, rows(y)], p_s.at[t], p_r.at[xh, y], device(2 * xl + t, y, z, k))
    sends.append(send(q_in, qb.at[xh, rows(z)], q_s.at[0, 0], q_r.at[xh, z], device(opposite, y, z, k)))
    for d in (1, 2, 3):
        to = device(x, y, turn(z, d), k)
        sends.append(send(idx_in, idx.at[:, rows(z)], i_s.at[d], i_r.at[z], to))
        sends.append(send(q_in, qb.at[xh, rows(z)], q_s.at[0, d], q_r.at[xh, z], to))
    table_rows = pl.ds(NB * R + pl.multiple_of(k * TR, TR), TR)
    local = []
    for s in range(2):
        def part(core):
            return t_in.at[rows(z, TR), pl.ds(pl.multiple_of((2 * s + core) * W, W), W)]
        sends.append(send(part(1 - k), pt.at[s, table_rows], t_s.at[0, s], t_s.at[1, s], sibling))
        own = pltpu.make_async_copy(part(k), pt.at[s, table_rows], t_s.at[2, s])
        own.start()
        local.append(own)
    qb[xh, rows(z)] = q_in[...]
    idx[:, rows(z)] = idx_in[...]
    for turn_s, s in enumerate((xh, far)):
        owner = 2 * s + xh
        @pl.when(owner == x)
        def _():
            pt[s, rows(y)] = p_in[...]
        @pl.when(owner != x)
        def _():
            arrive(pt.at[s, rows(y)], p_r.at[s, y])
        for d in (1, 2, 3):
            sends.append(send(pt.at[s, rows(y)], pt.at[s, rows(y)], p_s.at[2 + turn_s * 3 + d - 1], p_r.at[s, y],
                              device(x, turn(y, d), z, k)))
    arrive(qb.at[far, rows(z)], q_r.at[far, z])
    for d in (1, 2, 3):
        sends.append(send(qb.at[far, rows(z)], qb.at[far, rows(z)], q_s.at[1, d], q_r.at[far, z],
                          device(x, y, turn(z, d), k)))
    for d in (1, 2, 3):
        arrive(idx.at[:, rows(turn(z, d))], i_r.at[turn(z, d)])

    first = xh * 512 + z * TR
    place = lax.broadcasted_iota(jnp.int32, (2 * TR, NB * R), 0)
    ids = (place + first + jnp.where(place >= TR, 256 - TR, 0)).astype(F32)
    count = jnp.zeros((2 * TR, NB * R), F32)
    for n in range(7):
        count += (idx[n:n + 1, :] == ids).astype(F32)

    for d in (1, 2, 3):
        for s in (xh, far):
            arrive(qb.at[s, rows(turn(z, d))], q_r.at[s, turn(z, d)])
            arrive(pt.at[s, rows(turn(y, d))], p_r.at[s, turn(y, d)])
    other_rows = pl.ds(NB * R + pl.multiple_of((1 - k) * TR, TR), TR)
    for s in range(2):
        arrive(pt.at[s, other_rows], t_s.at[1, s])
        local[s].wait()

    nt = (((1,), (1,)), ((), ()))
    for i in range(COLS // R):
        total = lax.dot_general(pt[0, i * R:(i + 1) * R], qb[0], nt, preferred_element_type=F32)
        total += lax.dot_general(pt[1, i * R:(i + 1) * R], qb[1], nt, preferred_element_type=F32)
        s_own[i * R:(i + 1) * R] = total
        sends.append(send(s_own.at[pl.ds(i * R, R)], s_far.at[pl.ds(i * R, R)], c_s.at[i], c_r.at[i], sibling))
    top = jnp.full((1, NB * R), -jnp.inf, F32)
    hit = jnp.zeros((1, NB * R), F32)
    positive = idx[7:8, :]
    base = xh * 2048 + z * R

    def here(i):
        return (lax.broadcasted_iota(jnp.int32, (R, NB * R), 0) + base + i * 512).astype(F32) == positive

    for i in range(COLS // R):
        arrive(s_far.at[pl.ds(i * R, R)], c_r.at[i])
        total = (s_own[i * R:(i + 1) * R] + s_far[i * R:(i + 1) * R]) * factor
        e_buf[i * R:(i + 1) * R] = total
        if i < NB:
            hit += jnp.sum(jnp.where(here(i), total, 0.0), axis=0, keepdims=True)
        else:
            total = jnp.where(count > 0, total, -jnp.inf)
        top = jnp.maximum(top, jnp.max(total, axis=0, keepdims=True))
    mass = jnp.zeros((1, NB * R), F32)
    for i in range(COLS // R):
        if i < NB:
            e = jnp.exp(e_buf[i * R:(i + 1) * R] - top)
        else:
            e = count * jnp.exp(jnp.where(count > 0, e_buf[i * R:(i + 1) * R] - top, 0.0))
        e_buf[i * R:(i + 1) * R] = e
        mass += jnp.sum(e, axis=0, keepdims=True)
    me = xh * 4 + z
    stats[me, 0:1] = top
    stats[me, 1:2] = mass
    stats[me, 2:3] = hit
    for n in range(1, 8):
        dx, d = n // 4, n % 4
        sends.append(send(stats.at[me], stats.at[me], st_s.at[n], st_r.at[me],
                          device(lax.rem(x + 2 * dx, 4), y, turn(z, d), k)))
    for n in range(1, 8):
        dx, d = n // 4, n % 4
        slot = lax.rem(xh + dx, 2) * 4 + turn(z, d)
        arrive(stats.at[slot], st_r.at[slot])
    row_top = stats[0, 0:1]
    for n in range(1, 8):
        row_top = jnp.maximum(row_top, stats[n, 0:1])
    mass = jnp.zeros((1, NB * R), F32)
    hit = jnp.zeros((1, NB * R), F32)
    for n in range(8):
        mass += stats[n, 1:2] * jnp.exp(stats[n, 0:1] - row_top)
        hit += stats[n, 2:3]
    log_total = row_top + jnp.log(mass)
    loss_out[...] = jnp.broadcast_to(log_total - hit, (8, NB * R))
    weight = idx[8:9, :] * factor
    scale = weight * jnp.exp(top - log_total)
    for i in range(COLS // R):
        g = scale * e_buf[i * R:(i + 1) * R]
        if i < NB:
            g = g - jnp.where(here(i), weight, 0.0)
        grad[i * R:(i + 1) * R] = g.astype(BF16)

    tn = (((0,), (0,)), ((), ()))

    def query_part(s, zz):
        return lax.dot_general(grad[:, rows(zz)], pt[s], tn, preferred_element_type=F32)

    def passage_part(s, i):
        return lax.dot_general(grad[rows(i)], qb[s], (((1,), (0,)), ((), ())), preferred_element_type=F32)

    def tile_sends(step, s):
        for d in (1, 2, 3):
            zz, yy = turn(z, d), turn(y, d)
            qg_part[step, d] = query_part(s, zz).astype(BF16)
            sends.append(send(qg_part.at[step, d], rq.at[step, 4 - d], qg_s.at[step, d], qg_r.at[step, 4 - d],
                              device(x, y, zz, k)))
            pg_part[step, d] = passage_part(s, yy).astype(BF16)
            sends.append(send(pg_part.at[step, d], rp.at[step, 4 - d], pg_s.at[step, d], pg_r.at[step, 4 - d],
                              device(x, yy, z, k)))

    tile_sends(0, far)
    tile_sends(1, xh)
    for s in range(2):
        tg_part[s] = lax.dot_general(grad[NB * R:], qb[s], (((1,), (0,)), ((), ())),
                                     preferred_element_type=F32).astype(BF16)
    for n in range(8):
        dx, d = n // 4, n % 4
        xx, yy = lax.rem(xl + dx, 2), turn(y, d)
        src = tg_part.at[xx, :, pl.ds(pl.multiple_of(yy * CW, CW), CW)]
        slot = dx * 4 + (4 - d) % 4
        if n:
            sends.append(send(src, rt.at[slot], tg_s.at[n], tg_r.at[slot], device(2 * xh + xx, yy, z, k)))
        else:
            own = pltpu.make_async_copy(src, rt.at[0], tg_s.at[0])
            own.start()
            local.append(own)
    qx[...] = query_part(far, z).astype(BF16)
    qg_out[...] = query_part(xh, z)
    px[0] = passage_part(far, y)
    px[1] = passage_part(xh, y)

    for d in (1, 2, 3):
        arrive(rq.at[0, d], qg_r.at[0, d])
    rq[0, 0] = (qx[...].astype(F32) + rq[0, 1].astype(F32) + rq[0, 2].astype(F32) + rq[0, 3].astype(F32)).astype(BF16)
    sends.append(send(rq.at[0, 0], rqx, qx_s.at[0], qx_s.at[1], device(opposite, y, z, k)))
    for step, s in enumerate((far, xh)):
        owner = 2 * s + xh
        for d in (1, 2, 3):
            arrive(rp.at[step, d], pg_r.at[step, d])
        total = px[step] + rp[step, 1].astype(F32) + rp[step, 2].astype(F32) + rp[step, 3].astype(F32)
        rp[step, 0] = total.astype(BF16)
        @pl.when(owner == x)
        def _():
            rpx[xl] = rp[step, 0]
        @pl.when(owner != x)
        def _():
            send(rp.at[step, 0], rpx.at[xl], px_s.at[step], px_r.at[xl], device(owner, y, z, k))

    local[2].wait()
    for n in range(1, 8):
        arrive(rt.at[n], tg_r.at[n])
    total = rt[0].astype(F32)
    for n in range(1, 8):
        total += rt[n].astype(F32)
    dst_y = 2 * k + lax.div(y, 2)
    for core in range(2):
        for h in range(2):
            tsum[core, h] = total[core * TR:(core + 1) * TR, h * 128:(h + 1) * 128]
            dst_z = 2 * lax.rem(y, 2) + h
            mine = (dst_y == y) & (dst_z == z) & (k == core)
            @pl.when(mine)
            def _():
                tt[z] = tsum[core, h]
            @pl.when(jnp.logical_not(mine))
            def _():
                send(tsum.at[core, h], tt.at[z], tt_s.at[core, h], tt_r.at[z], device(x, dst_y, dst_z, core))

    for d in (1, 2, 3):
        arrive(rq.at[1, d], qg_r.at[1, d])
    qg_out[...] += rq[1, 1].astype(F32) + rq[1, 2].astype(F32) + rq[1, 3].astype(F32)
    for zz in range(4):
        @pl.when(jnp.logical_not((src_y == y) & (src_k == k) & (z == zz)))
        def _():
            arrive(tt.at[zz], tt_r.at[zz])
        tg_out[zz * TR:(zz + 1) * TR] = tt[zz]
    arrive(rqx, qx_s.at[1])
    qg_out[...] += rqx[...].astype(F32)
    for t in range(2):
        @pl.when(x != 2 * xl + t)
        def _():
            arrive(rpx.at[t], px_r.at[t])
    pg_out[...] = rpx[0].astype(F32) + rpx[1].astype(F32)

    for copy in sends:
        copy.wait_send()

    def left(src, ss):
        pltpu.make_async_remote_copy(
            src_ref=src, dst_ref=src, send_sem=ss, recv_sem=ss, device_id=sibling, device_id_type=MESH
        ).wait_send()

    for t in range(2):
        @pl.when(x != 2 * xl + t)
        def _():
            left(p_in, p_s.at[t])
    for step, s in enumerate((far, xh)):
        @pl.when(2 * s + xh != x)
        def _():
            left(rp.at[step, 0], px_s.at[step])
    for core in range(2):
        for h in range(2):
            mine = (dst_y == y) & (2 * lax.rem(y, 2) + h == z) & (k == core)
            @pl.when(jnp.logical_not(mine))
            def _():
                left(tsum.at[core, h], tt_s.at[core, h])


def per_device(queries, passages, table, neg_owner, neg_row, positive, loss_weight):
    factor = float(queries.shape[1] * 4) ** (-0.5)
    ids = (neg_owner * 256 + neg_row).astype(F32).T
    idx = jnp.concatenate(
        [ids, positive.astype(F32)[None], loss_weight[None], jnp.zeros((7, R), F32)], axis=0
    )
    vmem = pl.BlockSpec(memory_space=pltpu.VMEM)
    dma = pltpu.SemaphoreType.DMA
    loss, qg, pg, tg = pl.pallas_call(
        functools.partial(kernel, factor),
        name="contrastive",
        out_shape=(
            jax.ShapeDtypeStruct((8, NB * R), F32),
            jax.ShapeDtypeStruct((R, W), F32),
            jax.ShapeDtypeStruct((R, W), F32),
            jax.ShapeDtypeStruct((4 * TR, 128), F32),
        ),
        in_specs=[vmem, vmem, pl.BlockSpec(memory_space=pl.ANY), vmem],
        out_specs=[vmem] * 4,
        scratch_shapes=[
            pltpu.VMEM((2, NB * R, W), BF16),
            pltpu.VMEM((2, COLS, W), BF16),
            pltpu.VMEM((16, NB * R), F32),
            pltpu.VMEM((COLS, NB * R), F32),
            pltpu.VMEM((COLS, NB * R), F32),
            pltpu.VMEM((COLS, NB * R), F32),
            pltpu.VMEM((COLS, NB * R), BF16),
            pltpu.VMEM((8, 8, NB * R), F32),
            pltpu.VMEM((2, 4, R, W), BF16),
            pltpu.VMEM((2, 4, R, W), BF16),
            pltpu.VMEM((2, 2 * TR, W), BF16),
            pltpu.VMEM((2, 4, R, W), BF16),
            pltpu.VMEM((R, W), BF16),
            pltpu.VMEM((2, 4, R, W), BF16),
            pltpu.VMEM((2, R, W), BF16),
            pltpu.VMEM((8, 2 * TR, CW), BF16),
            pltpu.VMEM((4, TR, 128), F32),
            pltpu.VMEM((R, W), BF16),
            pltpu.VMEM((2, R, W), F32),
            pltpu.VMEM((2, 2, TR, 128), F32),
            dma((2, 4)), dma((2, 4)),
            dma((8,)), dma((2, 4)),
            dma((3, 2)),
            dma((4,)), dma((4,)),
            dma((5,)), dma((5,)),
            dma((8,)), dma((8,)),
            dma((2, 4)), dma((2, 4)),
            dma((2,)),
            dma((2, 4)), dma((2, 4)),
            dma((2,)), dma((2,)),
            dma((8,)), dma((8,)),
            dma((2, 2)), dma((4,)),
        ],
        compiler_params=pltpu.CompilerParams(
            collective_id=0, has_side_effects=True, vmem_limit_bytes=48 * 2**20
        ),
    )(queries, passages, table, idx)
    start = lax.rem(lax.axis_index("blk"), 4) * R + lax.axis_index("corpus") * 32
    return lax.dynamic_slice(loss[0], (start,), (32,)), qg, pg, tg


def solution(mesh):
    placed = (
        P("blk", "corpus"),
        P("blk", "corpus"),
        P("corpus", None),
        P("blk", None),
        P("blk", None),
        P("blk"),
        P("blk"),
    )
    return jax.shard_map(
        per_device,
        mesh=mesh,
        in_specs=placed,
        out_specs=(
            P(("blk", "corpus")),
            P("blk", "corpus"),
            P("blk", "corpus"),
            P("corpus", "blk"),
        ),
        check_vma=False,
    )
```

```python
import functools

import jax
import jax.numpy as jnp
from jax import lax
from jax.experimental import pallas as pl
from jax.experimental.pallas import tpu as pltpu
from jax.sharding import PartitionSpec as P

MESH = pl.DeviceIdType.MESH
F32 = jnp.float32
BF16 = jnp.bfloat16

R = 128
H = 64
W = 1024
NB = 4
TR = 64
COLS = NB * R + 2 * TR
CW = 256


def device(x, y, z, k):
    return (lax.rem(x, 2) * 16 + y * 4 + z, lax.div(x, 2) * 2 + k)


def kernel(
    factor, q_in, p_in, t_in, owner_in, row_in, pos_in, weight_in, loss_out, qg_out, pg_out, tg_out,
    qb, pt, idx, s_own, s_far, e_buf, grad, stats, qg_part, pg_part, tg_part,
    rq, rqx, rp, rpx, rt, rtx, tt, qx, px, tx, tsum, p_buf, owner_buf, row_buf, pos_buf, weight_buf, loss_row,
    in_s, q_s, q_r, px_s, p_s, p_r, t_s, i_s, i_r, c_s, c_r, st_s, st_r,
    qg_s, qg_r, qx_s, pg_s, pg_r, sx_s, sx_r, tx_s, tg_s, tg_r, tt_s, tt_r,
):
    b, c = lax.axis_index("blk"), lax.axis_index("corpus")
    xl, y, z = lax.div(b, 16), lax.rem(lax.div(b, 4), 4), lax.rem(b, 4)
    xh, k = lax.div(c, 2), lax.rem(c, 2)
    x = 2 * xh + xl
    far, yon = 1 - xh, 1 - xl
    opposite = 2 * far + xl
    sibling = device(x, y, z, 1 - k)

    def send(src, dst, ss, rs, where):
        copy = pltpu.make_async_remote_copy(
            src_ref=src, dst_ref=dst, send_sem=ss, recv_sem=rs, device_id=where, device_id_type=MESH
        )
        copy.start()
        sends.append(copy)

    def arrive(dst, rs):
        pltpu.make_async_remote_copy(
            src_ref=dst, dst_ref=dst, send_sem=rs, recv_sem=rs, device_id=sibling, device_id_type=MESH
        ).wait_recv()

    def stage(src, dst, sem):
        copy = pltpu.make_async_copy(src, dst, sem)
        copy.start()
        return copy

    def turn(v, d):
        return lax.rem(v + d, 4)

    def rows(i, n=R):
        return pl.ds(pl.multiple_of(i * n, n), n)

    def half(l, yy):
        return rows(l * 4 + yy, H)

    sends = []
    barrier = pltpu.get_barrier_semaphore()
    peers = [sibling]
    for d in (1, 2, 3):
        peers.append(device(turn(x, d), y, z, k))
        peers.append(device(x, turn(y, d), z, k))
        peers.append(device(x, y, turn(z, d), k))
    for peer in peers:
        pl.semaphore_signal(barrier, 1, device_id=peer, device_id_type=MESH)

    table_rows = pl.ds(NB * R + pl.multiple_of(k * TR, TR), TR)
    own = [
        stage(p_in, p_buf, in_s.at[0]),
        stage(q_in, qb.at[xh, rows(z)], in_s.at[1]),
        stage(owner_in, owner_buf, in_s.at[2]),
        stage(row_in, row_buf, in_s.at[3]),
        stage(pos_in, pos_buf, in_s.at[4]),
        stage(weight_in, weight_buf, in_s.at[5]),
    ]

    def table_part(s, core):
        return t_in.at[rows(z, TR), pl.ds(pl.multiple_of((2 * s + core) * W, W), W)]

    own_table = [stage(table_part(s, k), pt.at[s, table_rows], in_s.at[6 + s]) for s in range(2)]
    for copy in own:
        copy.wait()
    pt[xh, half(xl, y)] = p_buf[rows(xh, H)]
    idx[0:7, rows(z)] = (owner_buf[...] * 256 + row_buf[...]).astype(F32)
    idx[7:8, rows(z)] = pos_buf[...].astype(F32)
    idx[8:9, rows(z)] = weight_buf[...]
    pl.semaphore_wait(barrier, len(peers))

    send(p_buf.at[rows(xh, H)], pt.at[xh, half(xl, y)], px_s.at[0], p_r.at[xh, xl, y], device(2 * xh + yon, y, z, k))
    send(p_buf.at[rows(far, H)], pt.at[xh, half(xl, y)], px_s.at[1], p_r.at[xh, xl, y], device(2 * far + yon, y, z, k))
    send(p_buf.at[rows(far, H)], pt.at[xh, half(xl, y)], px_s.at[2], p_r.at[xh, xl, y], device(opposite, y, z, k))

    def spread_passages(n, s, l):
        for d in (1, 2, 3):
            send(pt.at[s, half(l, y)], pt.at[s, half(l, y)], p_s.at[n, d], p_r.at[s, l, y], device(x, turn(y, d), z, k))

    def spread_queries(n, s):
        for d in (1, 2, 3):
            send(qb.at[s, rows(z)], qb.at[s, rows(z)], q_s.at[n, d], q_r.at[s, z], device(x, y, turn(z, d), k))

    spread_passages(0, xh, xl)
    spread_queries(0, xh)
    send(qb.at[xh, rows(z)], qb.at[xh, rows(z)], q_s.at[0, 0], q_r.at[xh, z], device(opposite, y, z, k))
    for d in (1, 2, 3):
        send(idx.at[:, rows(z)], idx.at[:, rows(z)], i_s.at[d], i_r.at[z], device(x, y, turn(z, d), k))
    for s in range(2):
        send(table_part(s, 1 - k), pt.at[s, table_rows], t_s.at[0, s], t_s.at[1, s], sibling)
    for n, (s, l) in enumerate(((xh, yon), (far, yon), (far, xl))):
        arrive(pt.at[s, half(l, y)], p_r.at[s, l, y])
        spread_passages(n + 1, s, l)
    arrive(qb.at[far, rows(z)], q_r.at[far, z])
    spread_queries(1, far)
    for d in (1, 2, 3):
        arrive(idx.at[:, rows(turn(z, d))], i_r.at[turn(z, d)])

    first = xh * 512 + z * TR
    place = lax.broadcasted_iota(jnp.int32, (2 * TR, NB * R), 0)
    named = (place + first + jnp.where(place >= TR, 256 - TR, 0)).astype(F32)
    count = jnp.zeros((2 * TR, NB * R), F32)
    for n in range(7):
        count += (idx[n:n + 1, :] == named).astype(F32)

    other_rows = pl.ds(NB * R + pl.multiple_of((1 - k) * TR, TR), TR)
    for s in range(2):
        arrive(pt.at[s, other_rows], t_s.at[1, s])
        own_table[s].wait()
    nt = (((1,), (1,)), ((), ()))
    for s in (xh, far):
        for d in (1, 2, 3):
            arrive(qb.at[s, rows(turn(z, d))], q_r.at[s, turn(z, d)])
            for l in (xl, yon):
                arrive(pt.at[s, half(l, turn(y, d))], p_r.at[s, l, turn(y, d)])
        for i in range(COLS // R):
            term = lax.dot_general(pt[s, i * R:(i + 1) * R], qb[s], nt, preferred_element_type=F32)
            if s is xh:
                s_own[i * R:(i + 1) * R] = term
            else:
                s_own[i * R:(i + 1) * R] += term
                send(s_own.at[pl.ds(i * R, R)], s_far.at[pl.ds(i * R, R)], c_s.at[i], c_r.at[i], sibling)
    top = jnp.full((1, NB * R), -jnp.inf, F32)
    hit = jnp.zeros((1, NB * R), F32)
    positive = idx[7:8, :]

    def here(i):
        r = lax.broadcasted_iota(jnp.int32, (R, NB * R), 0)
        r = r + jnp.where(r >= H, 4 * R - H, 0) + (i // 2 * 2048 + i % 2 * 1024) + z * R + xh * H
        return r.astype(F32) == positive

    for i in range(COLS // R):
        arrive(s_far.at[pl.ds(i * R, R)], c_r.at[i])
        total = (s_own[i * R:(i + 1) * R] + s_far[i * R:(i + 1) * R]) * factor
        e_buf[i * R:(i + 1) * R] = total
        if i < NB:
            hit += jnp.sum(jnp.where(here(i), total, 0.0), axis=0, keepdims=True)
        else:
            total = jnp.where(count > 0, total, -jnp.inf)
        top = jnp.maximum(top, jnp.max(total, axis=0, keepdims=True))
    mass = jnp.zeros((1, NB * R), F32)
    for i in range(COLS // R):
        if i < NB:
            e = jnp.exp(e_buf[i * R:(i + 1) * R] - top)
        else:
            e = count * jnp.exp(jnp.where(count > 0, e_buf[i * R:(i + 1) * R] - top, 0.0))
        e_buf[i * R:(i + 1) * R] = e
        mass += jnp.sum(e, axis=0, keepdims=True)
    me = xh * 4 + z
    stats[me, 0:1] = top
    stats[me, 1:2] = mass
    stats[me, 2:3] = hit
    for n in range(1, 8):
        dx, d = n // 4, n % 4
        send(stats.at[me], stats.at[me], st_s.at[n], st_r.at[me], device(turn(x, 2 * dx), y, turn(z, d), k))
    for n in range(1, 8):
        dx, d = n // 4, n % 4
        slot = lax.rem(xh + dx, 2) * 4 + turn(z, d)
        arrive(stats.at[slot], st_r.at[slot])
    row_top = stats[0, 0:1]
    for n in range(1, 8):
        row_top = jnp.maximum(row_top, stats[n, 0:1])
    mass = jnp.zeros((1, NB * R), F32)
    hit = jnp.zeros((1, NB * R), F32)
    for n in range(8):
        mass += stats[n, 1:2] * jnp.exp(stats[n, 0:1] - row_top)
        hit += stats[n, 2:3]
    log_total = row_top + jnp.log(mass)
    loss_row[...] = log_total - hit
    own_loss = jnp.broadcast_to(loss_row[:, rows(z)], (8, R))
    loss_out[...] = pltpu.roll(own_loss, lax.rem(R - c * 32, R), 1)
    weight = idx[8:9, :] * factor
    scale = weight * jnp.exp(top - log_total)
    for i in range(COLS // R):
        g = scale * e_buf[i * R:(i + 1) * R]
        if i < NB:
            g = g - jnp.where(here(i), weight, 0.0)
        grad[i * R:(i + 1) * R] = g.astype(BF16)

    nn, tn = (((1,), (0,)), ((), ())), (((0,), (0,)), ((), ()))

    def query_part(s, zz):
        return lax.dot_general(grad[:, rows(zz)], pt[s], tn, preferred_element_type=F32)

    def query_sends(step, s):
        for d in (1, 2, 3):
            zz = turn(z, d)
            qg_part[step, d] = query_part(s, zz).astype(BF16)
            send(qg_part.at[step, d], rq.at[step, 4 - d], qg_s.at[step, d], qg_r.at[step, 4 - d], device(x, y, zz, k))

    def passage_sends(n, s, l):
        part = lax.dot_general(grad[rows(l, 4 * H)], qb[s], nn, preferred_element_type=F32)
        pg_part[n] = part.astype(BF16)
        px[n] = part
        for d in (1, 2, 3):
            yy = turn(y, d)
            send(pg_part.at[n, rows(yy, H)], rp.at[n, 4 - d], pg_s.at[n, d], pg_r.at[n, 4 - d], device(x, yy, z, k))

    def table_half(l):
        return lax.dot_general(grad[NB * R:], qb[l], nn, preferred_element_type=F32)

    order = ((far, xl), (far, yon), (xh, yon), (xh, xl))
    tg_part[0] = table_half(yon).astype(BF16)
    send(tg_part.at[0], rtx, tx_s.at[0], tx_s.at[1], device(2 * xh + yon, y, z, k))
    passage_sends(0, *order[0])
    query_sends(0, far)
    passage_sends(1, *order[1])
    passage_sends(2, *order[2])
    query_sends(1, xh)
    passage_sends(3, *order[3])
    tx[...] = table_half(xl)
    qx[...] = query_part(far, z)
    qg_out[...] = query_part(xh, z)

    arrive(rtx, tx_s.at[1])
    tx[...] += rtx[...].astype(F32)
    tg_part[1] = tx[...].astype(BF16)
    for d in (1, 2, 3):
        yy = turn(y, d)
        send(tg_part.at[1, :, rows(yy, CW)], rt.at[4 - d], tg_s.at[d], tg_r.at[4 - d], device(x, yy, z, k))

    def passage_sum(n):
        total = px[n, rows(y, H)]
        for d in (1, 2, 3):
            arrive(rp.at[n, d], pg_r.at[n, d])
            total += rp[n, d].astype(F32)
        return total

    def passage_on(n):
        s, l = order[n]
        rp[n, 0] = passage_sum(n).astype(BF16)
        send(rp.at[n, 0], rpx.at[xh, xl], sx_s.at[n], sx_r.at[xh, xl], device(2 * s + l, y, z, k))

    passage_on(0)
    total = qx[...]
    for d in (1, 2, 3):
        arrive(rq.at[0, d], qg_r.at[0, d])
        total += rq[0, d].astype(F32)
    rq[0, 0] = total.astype(BF16)
    send(rq.at[0, 0], rqx, qx_s.at[0], qx_s.at[1], device(opposite, y, z, k))
    passage_on(1)
    passage_on(2)

    total = tx[:, rows(y, CW)]
    for d in (1, 2, 3):
        arrive(rt.at[d], tg_r.at[d])
        total += rt[d].astype(F32)
    dst_y = 2 * k + lax.div(y, 2)
    for core in range(2):
        for h in range(2):
            tsum[core, h] = total[core * TR:(core + 1) * TR, h * 128:(h + 1) * 128]
            dst_z = 2 * lax.rem(y, 2) + h
            mine = (dst_y == y) & (dst_z == z) & (k == core)

            @pl.when(mine)
            def _():
                tt[z] = tsum[core, h]

            @pl.when(jnp.logical_not(mine))
            def _():
                send(tsum.at[core, h], tt.at[z], tt_s.at[core, h], tt_r.at[z], device(x, dst_y, dst_z, core))
                sends.pop()

    total = qg_out[...]
    for d in (1, 2, 3):
        arrive(rq.at[1, d], qg_r.at[1, d])
        total += rq[1, d].astype(F32)
    arrive(rqx, qx_s.at[1])
    qg_out[...] = total + rqx[...].astype(F32)
    total = passage_sum(3)
    arrive(rpx.at[xh, yon], sx_r.at[xh, yon])
    pg_out[rows(xh, H)] = total + rpx[xh, yon].astype(F32)
    for l in range(2):
        arrive(rpx.at[far, l], sx_r.at[far, l])
    pg_out[rows(far, H)] = rpx[far, 0].astype(F32) + rpx[far, 1].astype(F32)
    src_y = 2 * lax.rem(y, 2) + lax.div(z, 2)
    src_k = lax.div(y, 2)
    for zz in range(4):
        @pl.when(jnp.logical_not((src_y == y) & (src_k == k) & (z == zz)))
        def _():
            arrive(tt.at[zz], tt_r.at[zz])

        tg_out[zz * TR:(zz + 1) * TR] = tt[zz]

    for copy in sends:
        copy.wait_send()
    for core in range(2):
        for h in range(2):
            mine = (dst_y == y) & (2 * lax.rem(y, 2) + h == z) & (k == core)

            @pl.when(jnp.logical_not(mine))
            def _():
                src, sem = tsum.at[core, h], tt_s.at[core, h]
                pltpu.make_async_remote_copy(
                    src_ref=src, dst_ref=src, send_sem=sem, recv_sem=sem, device_id=sibling, device_id_type=MESH
                ).wait_send()


def place(loss_in, qg_in, pg_in, tg_in, loss_out, qg_out, pg_out, tg_out, sem):
    copies = []
    for n, (src, dst) in enumerate(((qg_in, qg_out), (pg_in, pg_out), (tg_in, tg_out))):
        copies.append(pltpu.make_async_copy(src, dst, sem.at[n]))
        copies[-1].start()
    loss_out[...] = loss_in[0:1, 0:32]
    for copy in copies:
        copy.wait()


def per_device(queries, passages, table, neg_owner, neg_row, positive, loss_weight):
    factor = float(queries.shape[1] * 4) ** (-0.5)
    vmem = pl.BlockSpec(memory_space=pltpu.VMEM)
    dma = pltpu.SemaphoreType.DMA
    loss, qg, pg, tg = pl.pallas_call(
        functools.partial(kernel, factor),
        name="contrastive",
        out_shape=(
            pltpu.VMEM((8, R), F32),
            pltpu.VMEM((R, W), F32),
            pltpu.VMEM((R, W), F32),
            pltpu.VMEM((4 * TR, 128), F32),
        ),
        in_specs=[pl.BlockSpec(memory_space=pl.ANY)] * 7,
        out_specs=[vmem] * 4,
        scratch_shapes=[
            pltpu.VMEM((2, NB * R, W), BF16),
            pltpu.VMEM((2, COLS, W), BF16),
            pltpu.VMEM((16, NB * R), F32),
            pltpu.VMEM((COLS, NB * R), F32),
            pltpu.VMEM((COLS, NB * R), F32),
            pltpu.VMEM((COLS, NB * R), F32),
            pltpu.VMEM((COLS, NB * R), BF16),
            pltpu.VMEM((8, 8, NB * R), F32),
            pltpu.VMEM((2, 4, R, W), BF16),
            pltpu.VMEM((4, 4 * H, W), BF16),
            pltpu.VMEM((2, 2 * TR, W), BF16),
            pltpu.VMEM((2, 4, R, W), BF16),
            pltpu.VMEM((R, W), BF16),
            pltpu.VMEM((4, 4, H, W), BF16),
            pltpu.VMEM((2, 2, H, W), BF16),
            pltpu.VMEM((4, 2 * TR, CW), BF16),
            pltpu.VMEM((2 * TR, W), BF16),
            pltpu.VMEM((4, TR, 128), F32),
            pltpu.VMEM((R, W), F32),
            pltpu.VMEM((4, 4 * H, W), F32),
            pltpu.VMEM((2 * TR, W), F32),
            pltpu.VMEM((2, 2, TR, 128), F32),
            pltpu.VMEM((R, W), BF16),
            pltpu.VMEM((7, R), jnp.int32),
            pltpu.VMEM((7, R), jnp.int32),
            pltpu.VMEM((1, R), jnp.int32),
            pltpu.VMEM((1, R), F32),
            pltpu.VMEM((1, NB * R), F32),
            dma((8,)),
            dma((2, 4)), dma((2, 4)),
            dma((3,)), dma((4, 4)), dma((2, 2, 4)),
            dma((2, 2)),
            dma((4,)), dma((4,)),
            dma((5,)), dma((5,)),
            dma((8,)), dma((8,)),
            dma((2, 4)), dma((2, 4)),
            dma((2,)),
            dma((4, 4)), dma((4, 4)),
            dma((3,)), dma((2, 2)),
            dma((2,)), dma((4,)), dma((4,)),
            dma((2, 2)), dma((4,)),
        ],
        compiler_params=pltpu.CompilerParams(
            collective_id=0, has_side_effects=True, vmem_limit_bytes=48 * 2**20
        ),
    )(*[
        pltpu.with_memory_space_constraint(a, pltpu.HBM)
        for a in (queries, passages, table, neg_owner.T, neg_row.T, positive[None], loss_weight[None])
    ])
    loss, qg, pg, tg = pl.pallas_call(
        place,
        name="place",
        out_shape=(
            jax.ShapeDtypeStruct((1, 32), F32),
            jax.ShapeDtypeStruct((R, W), F32),
            jax.ShapeDtypeStruct((R, W), F32),
            jax.ShapeDtypeStruct((4 * TR, 128), F32),
        ),
        in_specs=[vmem] + [pl.BlockSpec(memory_space=pl.ANY)] * 3,
        out_specs=[vmem] + [pl.BlockSpec(memory_space=pl.ANY)] * 3,
        scratch_shapes=[dma((3,))],
    )(*[pltpu.with_memory_space_constraint(a, pltpu.VMEM) for a in (loss, qg, pg, tg)])
    return loss[0], qg, pg, tg


def solution(mesh):
    placed = (
        P("blk", "corpus"),
        P("blk", "corpus"),
        P("corpus", None),
        P("blk", None),
        P("blk", None),
        P("blk"),
        P("blk"),
    )
    return jax.shard_map(
        per_device,
        mesh=mesh,
        in_specs=placed,
        out_specs=(
            P(("blk", "corpus")),
            P("blk", "corpus"),
            P("blk", "corpus"),
            P("corpus", "blk"),
        ),
        check_vma=False,
    )
```

```python
import functools

import jax
import jax.numpy as jnp
from jax import lax
from jax.experimental import pallas as pl
from jax.experimental.pallas import tpu as pltpu
from jax.sharding import PartitionSpec as P

MESH = pl.DeviceIdType.MESH
F32 = jnp.float32
BF16 = jnp.bfloat16

R = 128
H = 64
W = 1024
NB = 4
TR = 64
COLS = NB * R + 2 * TR
CW = 256


def device(x, y, z, k):
    return (lax.rem(x, 2) * 16 + y * 4 + z, lax.div(x, 2) * 2 + k)


def kernel(
    factor, q_in, p_in, t_in, owner_in, row_in, pos_in, weight_in, loss_out, qg_out, pg_out, tg_out,
    qb, pt, idx, s_own, s_far, e_buf, grad, stats, qg_part, pg_part, tg_part,
    qg_on, pg_on, rqa, rpa, qg_sum, pg_sum, rq, rqx, rp, rpx, rt, rtx, tt, qx, px, tx, tsum, p_buf, owner_buf, row_buf, pos_buf, weight_buf, loss_row,
    in_s, q_s, q_r, px_s, px_r, p_s, p_r, t_s, i_s, i_r, c_s, c_r, st_s, st_r,
    qg_s, qg_r, qx_s, pg_s, pg_r, sx_s, sx_r, tx_s, tg_s, tg_r, tt_s, tt_r,
):
    b, c = lax.axis_index("blk"), lax.axis_index("corpus")
    xl, y, z = lax.div(b, 16), lax.rem(lax.div(b, 4), 4), lax.rem(b, 4)
    xh, k = lax.div(c, 2), lax.rem(c, 2)
    x = 2 * xh + xl
    far, yon = 1 - xh, 1 - xl
    opposite = 2 * far + xl
    sibling = device(x, y, z, 1 - k)

    def send(src, dst, ss, rs, where):
        copy = pltpu.make_async_remote_copy(
            src_ref=src, dst_ref=dst, send_sem=ss, recv_sem=rs, device_id=where, device_id_type=MESH
        )
        copy.start()
        sends.append(copy)

    def arrive(dst, rs):
        pltpu.make_async_remote_copy(
            src_ref=dst, dst_ref=dst, send_sem=rs, recv_sem=rs, device_id=sibling, device_id_type=MESH
        ).wait_recv()

    def stage(src, dst, sem):
        copy = pltpu.make_async_copy(src, dst, sem)
        copy.start()
        return copy

    def turn(v, d):
        return lax.rem(v + d, 4)

    def rows(i, n=R):
        return pl.ds(pl.multiple_of(i * n, n), n)

    def half(l, yy):
        return rows(l * 4 + yy, H)

    sends = []
    barrier = pltpu.get_barrier_semaphore()
    peers = [sibling]
    for d in (1, 2, 3):
        peers.append(device(turn(x, d), y, z, k))
        peers.append(device(x, turn(y, d), z, k))
        peers.append(device(x, y, turn(z, d), k))
    for peer in peers:
        pl.semaphore_signal(barrier, 1, device_id=peer, device_id_type=MESH)

    table_rows = pl.ds(NB * R + pl.multiple_of(k * TR, TR), TR)
    own = [
        stage(p_in, p_buf, in_s.at[0]),
        stage(q_in, qb.at[xh, rows(z)], in_s.at[1]),
        stage(owner_in, owner_buf, in_s.at[2]),
        stage(row_in, row_buf, in_s.at[3]),
        stage(pos_in, pos_buf, in_s.at[4]),
        stage(weight_in, weight_buf, in_s.at[5]),
    ]

    def table_part(s, core):
        return t_in.at[rows(z, TR), pl.ds(pl.multiple_of((2 * s + core) * W, W), W)]

    own_table = [stage(table_part(s, k), pt.at[s, table_rows], in_s.at[6 + s]) for s in range(2)]
    for copy in own:
        copy.wait()
    pt[xh, half(xl, y)] = p_buf[rows(xh, H)]
    idx[0:7, rows(z)] = (owner_buf[...] * 256 + row_buf[...]).astype(F32)
    idx[7:8, rows(z)] = pos_buf[...].astype(F32)
    idx[8:9, rows(z)] = weight_buf[...]
    pl.semaphore_wait(barrier, len(peers))

    def passages(s, l, d, part=None):
        return pt.at[s, half(l, turn(y, d)) if part is None else rows((l * 4 + turn(y, d)) * 2 + part, H // 2)]

    def queries(s, d, part=None):
        return qb.at[s, rows(turn(z, d)) if part is None else rows(turn(z, d) * 2 + part, R // 2)]

    def spread(block, ss, rs, forward, back):
        send(block(0), block(0), ss.at[1], rs.at[1], forward)
        send(block(0), block(0), ss.at[3], rs.at[3], back)

    def relay(block, ss, rs, forward, back):
        arrive(block(3), rs.at[1])
        send(block(3, 0), block(3, 0), ss.at[0], rs.at[0], forward)
        arrive(block(1), rs.at[3])
        send(block(1, 1), block(1, 1), ss.at[2], rs.at[2], back)

    def finish(block, rs):
        arrive(block(2, 0), rs.at[0])
        arrive(block(2, 1), rs.at[2])

    y_next, y_last = device(x, turn(y, 1), z, k), device(x, turn(y, 3), z, k)
    z_next, z_last = device(x, y, turn(z, 1), k), device(x, y, turn(z, 3), k)

    def on_y(step, s, l):
        step(functools.partial(passages, s, l), p_s.at[s, l], p_r.at[s, l], y_next, y_last)

    def on_z(step, s):
        step(functools.partial(queries, s), q_s.at[s], q_r.at[s], z_next, z_last)

    def first_sends():
        mine = pt.at[xh, half(xl, y)]
        send(p_buf.at[rows(xh, H)], mine, px_s.at[0], px_r.at[xh, xl], device(2 * xh + yon, y, z, k))
        send(p_buf.at[rows(far, H)], mine, px_s.at[1], px_r.at[xh, xl], device(2 * far + yon, y, z, k))
        on_y(spread, xh, xl)
        on_z(spread, xh)
        send(queries(xh, 0), queries(xh, 0), qx_s.at[2], qx_s.at[3], device(opposite, y, z, k))
        send(p_buf.at[rows(far, H)], mine, px_s.at[2], px_r.at[xh, xl], device(opposite, y, z, k))

    first_sends()
    for d in (1, 2, 3):
        send(idx.at[:, rows(z)], idx.at[:, rows(z)], i_s.at[d], i_r.at[z], device(x, y, turn(z, d), k))
    for s in range(2):
        send(table_part(s, 1 - k), pt.at[s, table_rows], t_s.at[0, s], t_s.at[1, s], sibling)
    for s in (xh, far):
        arrive(passages(s, yon, 0), px_r.at[s, yon])
        on_y(spread, s, yon)
    on_y(relay, xh, xl)
    on_z(relay, xh)
    on_y(relay, xh, yon)
    arrive(queries(far, 0), qx_s.at[3])
    on_z(spread, far)
    on_y(relay, far, yon)
    arrive(passages(far, xl, 0), px_r.at[far, xl])
    on_y(spread, far, xl)
    for d in (1, 2, 3):
        arrive(idx.at[:, rows(turn(z, d))], i_r.at[turn(z, d)])

    first = xh * 512 + z * TR
    place = lax.broadcasted_iota(jnp.int32, (2 * TR, NB * R), 0)
    named = (place + first + jnp.where(place >= TR, 256 - TR, 0)).astype(F32)
    count = jnp.zeros((2 * TR, NB * R), F32)
    for n in range(7):
        count += (idx[n:n + 1, :] == named).astype(F32)

    other_rows = pl.ds(NB * R + pl.multiple_of((1 - k) * TR, TR), TR)
    for s in range(2):
        arrive(pt.at[s, other_rows], t_s.at[1, s])
        own_table[s].wait()
    nt = (((1,), (1,)), ((), ()))

    def logits_part(s, i):
        return lax.dot_general(pt[s, i * R:(i + 1) * R], qb[s], nt, preferred_element_type=F32)

    finish(functools.partial(queries, xh), q_r.at[xh])
    for l in (xl, yon):
        finish(functools.partial(passages, xh, l), p_r.at[xh, l])
    for i in range(2):
        s_own[i * R:(i + 1) * R] = logits_part(xh, i)
    on_z(relay, far)
    on_y(relay, far, xl)
    for i in range(2, COLS // R):
        s_own[i * R:(i + 1) * R] = logits_part(xh, i)
    finish(functools.partial(queries, far), q_r.at[far])
    for l in (yon, xl):
        finish(functools.partial(passages, far, l), p_r.at[far, l])
    for i in range(COLS // R):
        s_own[i * R:(i + 1) * R] += logits_part(far, i)
        send(s_own.at[pl.ds(i * R, R)], s_far.at[pl.ds(i * R, R)], c_s.at[i], c_r.at[i], sibling)
    top = jnp.full((1, NB * R), -jnp.inf, F32)
    hit = jnp.zeros((1, NB * R), F32)
    positive = idx[7:8, :]

    def here(i):
        r = lax.broadcasted_iota(jnp.int32, (R, NB * R), 0)
        r = r + jnp.where(r >= H, 4 * R - H, 0) + (i // 2 * 2048 + i % 2 * 1024) + z * R + xh * H
        return r.astype(F32) == positive

    for i in range(COLS // R):
        arrive(s_far.at[pl.ds(i * R, R)], c_r.at[i])
        total = (s_own[i * R:(i + 1) * R] + s_far[i * R:(i + 1) * R]) * factor
        e_buf[i * R:(i + 1) * R] = total
        if i < NB:
            hit += jnp.sum(jnp.where(here(i), total, 0.0), axis=0, keepdims=True)
        else:
            total = jnp.where(count > 0, total, -jnp.inf)
        top = jnp.maximum(top, jnp.max(total, axis=0, keepdims=True))
    mass = jnp.zeros((1, NB * R), F32)
    for i in range(COLS // R):
        if i < NB:
            e = jnp.exp(e_buf[i * R:(i + 1) * R] - top)
        else:
            e = count * jnp.exp(jnp.where(count > 0, e_buf[i * R:(i + 1) * R] - top, 0.0))
        e_buf[i * R:(i + 1) * R] = e
        mass += jnp.sum(e, axis=0, keepdims=True)
    me = xh * 4 + z
    stats[me, 0:1] = top
    stats[me, 1:2] = mass
    stats[me, 2:3] = hit
    for n in range(1, 8):
        dx, d = n // 4, n % 4
        send(stats.at[me], stats.at[me], st_s.at[n], st_r.at[me], device(turn(x, 2 * dx), y, turn(z, d), k))
    for n in range(1, 8):
        dx, d = n // 4, n % 4
        slot = lax.rem(xh + dx, 2) * 4 + turn(z, d)
        arrive(stats.at[slot], st_r.at[slot])
    row_top = stats[0, 0:1]
    for n in range(1, 8):
        row_top = jnp.maximum(row_top, stats[n, 0:1])
    mass = jnp.zeros((1, NB * R), F32)
    hit = jnp.zeros((1, NB * R), F32)
    for n in range(8):
        mass += stats[n, 1:2] * jnp.exp(stats[n, 0:1] - row_top)
        hit += stats[n, 2:3]
    log_total = row_top + jnp.log(mass)
    loss_row[...] = log_total - hit
    own_loss = jnp.broadcast_to(loss_row[:, rows(z)], (8, R))
    loss_out[...] = pltpu.roll(own_loss, lax.rem(R - c * 32, R), 1)
    weight = idx[8:9, :] * factor
    scale = weight * jnp.exp(top - log_total)
    for i in range(COLS // R):
        g = scale * e_buf[i * R:(i + 1) * R]
        if i < NB:
            g = g - jnp.where(here(i), weight, 0.0)
        grad[i * R:(i + 1) * R] = g.astype(BF16)

    nn, tn = (((1,), (0,)), ((), ())), (((0,), (0,)), ((), ()))

    def query_part(s, zz):
        return lax.dot_general(grad[:, rows(zz)], pt[s], tn, preferred_element_type=F32)

    def query_ahead(n, s):
        qg_part[n] = query_part(s, turn(z, 2)).astype(BF16)
        send(qg_part.at[n, pl.ds(0, H)], rqa.at[n, 0], qg_s.at[n, 0], qg_r.at[n, 0], z_next)
        send(qg_part.at[n, pl.ds(H, H)], rqa.at[n, 1], qg_s.at[n, 1], qg_r.at[n, 1], z_last)

    def query_next(n, s):
        for way, (d, to) in enumerate(((1, z_next), (3, z_last))):
            part = query_part(s, turn(z, d))
            arrive(rqa.at[n, way], qg_r.at[n, way])
            a, o = way * H, (1 - way) * H
            qg_on[n, way, a:a + H] = (part[a:a + H] + rqa[n, way].astype(F32)).astype(BF16)
            qg_on[n, way, o:o + H] = part[o:o + H].astype(BF16)
            send(qg_on.at[n, way], rq.at[n, way], qg_s.at[n, 2 + way], qg_r.at[n, 2 + way], to)

    def query_sum(n, total):
        for way in range(2):
            arrive(rq.at[n, way], qg_r.at[n, 2 + way])
            total += rq[n, way].astype(F32)
        return total

    Q = H // 2

    def passage_ahead(n):
        s, l = order[n]
        px[n] = lax.dot_general(grad[rows(l, 4 * H)], qb[s], nn, preferred_element_type=F32)
        pg_part[n] = px[n, rows(turn(y, 2), H)].astype(BF16)
        send(pg_part.at[n, pl.ds(0, Q)], rpa.at[n, 0], pg_s.at[n, 0], pg_r.at[n, 0], y_next)
        send(pg_part.at[n, pl.ds(Q, Q)], rpa.at[n, 1], pg_s.at[n, 1], pg_r.at[n, 1], y_last)

    def passage_next(n):
        for way, (d, to) in enumerate(((1, y_next), (3, y_last))):
            part = px[n, rows(turn(y, d), H)]
            arrive(rpa.at[n, way], pg_r.at[n, way])
            a, o = way * Q, (1 - way) * Q
            pg_on[n, way, a:a + Q] = (part[a:a + Q] + rpa[n, way].astype(F32)).astype(BF16)
            pg_on[n, way, o:o + Q] = part[o:o + Q].astype(BF16)
            send(pg_on.at[n, way], rp.at[n, way], pg_s.at[n, 2 + way], pg_r.at[n, 2 + way], to)

    def passage_sum(n):
        total = px[n, rows(y, H)]
        for way in range(2):
            arrive(rp.at[n, way], pg_r.at[n, 2 + way])
            total += rp[n, way].astype(F32)
        return total

    def passage_on(n):
        s, l = order[n]
        pg_sum[n] = passage_sum(n).astype(BF16)
        send(pg_sum.at[n], rpx.at[xh, xl], sx_s.at[n], sx_r.at[xh, xl], device(2 * s + l, y, z, k))

    def table_half(l):
        return lax.dot_general(grad[NB * R:], qb[l], nn, preferred_element_type=F32)

    order = ((far, xl), (far, yon), (xh, yon), (xh, xl))
    tg_part[0] = table_half(yon).astype(BF16)
    send(tg_part.at[0], rtx, tx_s.at[0], tx_s.at[1], device(2 * xh + yon, y, z, k))
    passage_ahead(0)
    query_ahead(0, far)
    passage_ahead(1)
    passage_ahead(2)
    query_ahead(1, xh)
    passage_ahead(3)
    tx[...] = table_half(xl)
    passage_next(0)
    query_next(0, far)
    passage_next(1)

    arrive(rtx, tx_s.at[1])
    tx[...] += rtx[...].astype(F32)
    tg_part[1] = tx[...].astype(BF16)
    for d in (1, 2, 3):
        yy = turn(y, d)
        send(tg_part.at[1, :, rows(yy, CW)], rt.at[4 - d], tg_s.at[d], tg_r.at[4 - d], device(x, yy, z, k))

    query_next(1, xh)
    passage_next(2)
    passage_next(3)
    qx[...] = query_part(far, z)
    passage_on(0)
    qg_sum[...] = query_sum(0, qx[...]).astype(BF16)
    send(qg_sum, rqx, qx_s.at[0], qx_s.at[1], device(opposite, y, z, k))
    passage_on(1)
    qg_out[...] = query_part(xh, z)

    total = tx[:, rows(y, CW)]
    for d in (1, 2, 3):
        arrive(rt.at[d], tg_r.at[d])
        total += rt[d].astype(F32)
    dst_y = 2 * k + lax.div(y, 2)
    for core in range(2):
        for h in range(2):
            tsum[core, h] = total[core * TR:(core + 1) * TR, h * 128:(h + 1) * 128]
            dst_z = 2 * lax.rem(y, 2) + h
            mine = (dst_y == y) & (dst_z == z) & (k == core)

            @pl.when(mine)
            def _():
                tt[z] = tsum[core, h]

            @pl.when(jnp.logical_not(mine))
            def _():
                send(tsum.at[core, h], tt.at[z], tt_s.at[core, h], tt_r.at[z], device(x, dst_y, dst_z, core))
                sends.pop()

    passage_on(2)
    total = query_sum(1, qg_out[...])
    arrive(rqx, qx_s.at[1])
    qg_out[...] = total + rqx[...].astype(F32)
    total = passage_sum(3)
    arrive(rpx.at[xh, yon], sx_r.at[xh, yon])
    pg_out[rows(xh, H)] = total + rpx[xh, yon].astype(F32)
    for l in range(2):
        arrive(rpx.at[far, l], sx_r.at[far, l])
    pg_out[rows(far, H)] = rpx[far, 0].astype(F32) + rpx[far, 1].astype(F32)
    src_y = 2 * lax.rem(y, 2) + lax.div(z, 2)
    src_k = lax.div(y, 2)
    for zz in range(4):
        @pl.when(jnp.logical_not((src_y == y) & (src_k == k) & (z == zz)))
        def _():
            arrive(tt.at[zz], tt_r.at[zz])

        tg_out[zz * TR:(zz + 1) * TR] = tt[zz]

    for copy in sends:
        copy.wait_send()
    for core in range(2):
        for h in range(2):
            mine = (dst_y == y) & (2 * lax.rem(y, 2) + h == z) & (k == core)

            @pl.when(jnp.logical_not(mine))
            def _():
                src, sem = tsum.at[core, h], tt_s.at[core, h]
                pltpu.make_async_remote_copy(
                    src_ref=src, dst_ref=src, send_sem=sem, recv_sem=sem, device_id=sibling, device_id_type=MESH
                ).wait_send()


def place(loss_in, qg_in, pg_in, tg_in, loss_out, qg_out, pg_out, tg_out, sem):
    copies = []
    for n, (src, dst) in enumerate(((qg_in, qg_out), (pg_in, pg_out), (tg_in, tg_out))):
        copies.append(pltpu.make_async_copy(src, dst, sem.at[n]))
        copies[-1].start()
    loss_out[...] = loss_in[0:1, 0:32]
    for copy in copies:
        copy.wait()


def per_device(queries, passages, table, neg_owner, neg_row, positive, loss_weight):
    factor = float(queries.shape[1] * 4) ** (-0.5)
    vmem = pl.BlockSpec(memory_space=pltpu.VMEM)
    dma = pltpu.SemaphoreType.DMA
    loss, qg, pg, tg = pl.pallas_call(
        functools.partial(kernel, factor),
        name="contrastive",
        out_shape=(
            pltpu.VMEM((8, R), F32),
            pltpu.VMEM((R, W), F32),
            pltpu.VMEM((R, W), F32),
            pltpu.VMEM((4 * TR, 128), F32),
        ),
        in_specs=[pl.BlockSpec(memory_space=pl.ANY)] * 7,
        out_specs=[vmem] * 4,
        scratch_shapes=[
            pltpu.VMEM((2, NB * R, W), BF16),
            pltpu.VMEM((2, COLS, W), BF16),
            pltpu.VMEM((16, NB * R), F32),
            pltpu.VMEM((COLS, NB * R), F32),
            pltpu.VMEM((COLS, NB * R), F32),
            pltpu.VMEM((COLS, NB * R), F32),
            pltpu.VMEM((COLS, NB * R), BF16),
            pltpu.VMEM((8, 8, NB * R), F32),
            pltpu.VMEM((2, R, W), BF16),
            pltpu.VMEM((4, H, W), BF16),
            pltpu.VMEM((2, 2 * TR, W), BF16),
            pltpu.VMEM((2, 2, R, W), BF16),
            pltpu.VMEM((4, 2, H, W), BF16),
            pltpu.VMEM((2, 2, H, W), BF16),
            pltpu.VMEM((4, 2, H // 2, W), BF16),
            pltpu.VMEM((R, W), BF16),
            pltpu.VMEM((3, H, W), BF16),
            pltpu.VMEM((2, 2, R, W), BF16),
            pltpu.VMEM((R, W), BF16),
            pltpu.VMEM((4, 2, H, W), BF16),
            pltpu.VMEM((2, 2, H, W), BF16),
            pltpu.VMEM((4, 2 * TR, CW), BF16),
            pltpu.VMEM((2 * TR, W), BF16),
            pltpu.VMEM((4, TR, 128), F32),
            pltpu.VMEM((R, W), F32),
            pltpu.VMEM((4, 4 * H, W), F32),
            pltpu.VMEM((2 * TR, W), F32),
            pltpu.VMEM((2, 2, TR, 128), F32),
            pltpu.VMEM((R, W), BF16),
            pltpu.VMEM((7, R), jnp.int32),
            pltpu.VMEM((7, R), jnp.int32),
            pltpu.VMEM((1, R), jnp.int32),
            pltpu.VMEM((1, R), F32),
            pltpu.VMEM((1, NB * R), F32),
            dma((8,)),
            dma((2, 4)), dma((2, 4)),
            dma((3,)), dma((2, 2)), dma((2, 2, 4)), dma((2, 2, 4)),
            dma((2, 2)),
            dma((4,)), dma((4,)),
            dma((5,)), dma((5,)),
            dma((8,)), dma((8,)),
            dma((2, 4)), dma((2, 4)),
            dma((4,)),
            dma((4, 4)), dma((4, 4)),
            dma((3,)), dma((2, 2)),
            dma((2,)), dma((4,)), dma((4,)),
            dma((2, 2)), dma((4,)),
        ],
        compiler_params=pltpu.CompilerParams(
            collective_id=0, has_side_effects=True, vmem_limit_bytes=48 * 2**20
        ),
    )(*[
        pltpu.with_memory_space_constraint(a, pltpu.HBM)
        for a in (queries, passages, table, neg_owner.T, neg_row.T, positive[None], loss_weight[None])
    ])
    loss, qg, pg, tg = pl.pallas_call(
        place,
        name="place",
        out_shape=(
            jax.ShapeDtypeStruct((1, 32), F32),
            jax.ShapeDtypeStruct((R, W), F32),
            jax.ShapeDtypeStruct((R, W), F32),
            jax.ShapeDtypeStruct((4 * TR, 128), F32),
        ),
        in_specs=[vmem] + [pl.BlockSpec(memory_space=pl.ANY)] * 3,
        out_specs=[vmem] + [pl.BlockSpec(memory_space=pl.ANY)] * 3,
        scratch_shapes=[dma((3,))],
    )(*[pltpu.with_memory_space_constraint(a, pltpu.VMEM) for a in (loss, qg, pg, tg)])
    return loss[0], qg, pg, tg


def solution(mesh):
    placed = (
        P("blk", "corpus"),
        P("blk", "corpus"),
        P("corpus", None),
        P("blk", None),
        P("blk", None),
        P("blk"),
        P("blk"),
    )
    return jax.shard_map(
        per_device,
        mesh=mesh,
        in_specs=placed,
        out_specs=(
            P(("blk", "corpus")),
            P("blk", "corpus"),
            P("blk", "corpus"),
            P("corpus", "blk"),
        ),
        check_vma=False,
    )
```

```python
import functools

import jax
import jax.numpy as jnp
from jax import lax
from jax.experimental import pallas as pl
from jax.experimental.pallas import tpu as pltpu
from jax.sharding import PartitionSpec as P

MESH = pl.DeviceIdType.MESH
F32 = jnp.float32
BF16 = jnp.bfloat16

R = 128
H = 64
W = 1024
NB = 4
TR = 64
COLS = NB * R + 2 * TR
CW = 256


def device(x, y, z, k):
    return (lax.rem(x, 2) * 16 + y * 4 + z, lax.div(x, 2) * 2 + k)


def kernel(
    factor, q_in, p_in, t_in, owner_in, row_in, pos_in, weight_in, loss_out, qg_out, pg_out, tg_out,
    qb, pt, idx, s_own, s_far, e_buf, grad, stats, hits, counts, qg_part, pg_part, tg_part,
    qg_on, pg_on, rqa, rpa, qg_sum, pg_sum, rq, rqx, rp, rpx, rt, rtx, tt, qx, px, tx, tsum, p_buf, owner_buf, row_buf, pos_buf, weight_buf, sums,
    in_s, q_s, q_r, qf_s, qf_r, px_s, px_r, p_s, p_r, t_s, i_s, i_r, c_s, c_r, st_s, st_r,
    qg_s, qg_r, qx_s, pg_s, pg_r, sx_s, sx_r, tx_s, tg_s, tg_r, tt_s, tt_r,
):
    b, c = lax.axis_index("blk"), lax.axis_index("corpus")
    xl, y, z = lax.div(b, 16), lax.rem(lax.div(b, 4), 4), lax.rem(b, 4)
    xh, k = lax.div(c, 2), lax.rem(c, 2)
    x = 2 * xh + xl
    far, yon = 1 - xh, 1 - xl
    opposite = 2 * far + xl
    sibling = device(x, y, z, 1 - k)

    def send(src, dst, ss, rs, where):
        copy = pltpu.make_async_remote_copy(
            src_ref=src, dst_ref=dst, send_sem=ss, recv_sem=rs, device_id=where, device_id_type=MESH
        )
        copy.start()
        sends.append(copy)

    def arrive(dst, rs):
        pltpu.make_async_remote_copy(
            src_ref=dst, dst_ref=dst, send_sem=rs, recv_sem=rs, device_id=sibling, device_id_type=MESH
        ).wait_recv()

    def stage(src, dst, sem):
        copy = pltpu.make_async_copy(src, dst, sem)
        copy.start()
        return copy

    def turn(v, d):
        return lax.rem(v + d, 4)

    def rows(i, n=R):
        return pl.ds(pl.multiple_of(i * n, n), n)

    def half(l, yy):
        return rows(l * 4 + yy, H)

    sends = []
    barrier = pltpu.get_barrier_semaphore()
    peers = [sibling]
    for d in (1, 2, 3):
        peers.append(device(turn(x, d), y, z, k))
        peers.append(device(x, turn(y, d), z, k))
        peers.append(device(x, y, turn(z, d), k))
    for peer in peers:
        pl.semaphore_signal(barrier, 1, device_id=peer, device_id_type=MESH)

    table_rows = pl.ds(NB * R + pl.multiple_of(k * TR, TR), TR)
    own = [
        stage(p_in, p_buf, in_s.at[0]),
        stage(q_in, qb.at[xh, rows(z)], in_s.at[1]),
        stage(owner_in, owner_buf, in_s.at[2]),
        stage(row_in, row_buf, in_s.at[3]),
        stage(pos_in, pos_buf, in_s.at[4]),
        stage(weight_in, weight_buf, in_s.at[5]),
    ]

    def table_part(s, core):
        return t_in.at[rows(z, TR), pl.ds(pl.multiple_of((2 * s + core) * W, W), W)]

    own_table = [stage(table_part(s, k), pt.at[s, table_rows], in_s.at[6 + s]) for s in range(2)]
    for copy in own:
        copy.wait()
    pt[xh, half(xl, y)] = p_buf[rows(xh, H)]
    idx[0:7, rows(z)] = (owner_buf[...] * 256 + row_buf[...]).astype(F32)
    idx[7:8, rows(z)] = pos_buf[...].astype(F32)
    idx[8:9, rows(z)] = weight_buf[...]
    pl.semaphore_wait(barrier, len(peers))

    def passages(s, l, d, part=None):
        return pt.at[s, half(l, turn(y, d)) if part is None else rows((l * 4 + turn(y, d)) * 2 + part, H // 2)]

    def queries(s, c, d, part=None):
        n = turn(z, d) * 2 + c
        return qb.at[s, rows(n, H) if part is None else rows(n * 2 + part, H // 2)]

    def spread(block, ss, rs, forward, back):
        send(block(0), block(0), ss.at[1], rs.at[1], forward)
        send(block(0), block(0), ss.at[3], rs.at[3], back)

    def relay(block, ss, rs, forward, back):
        arrive(block(3), rs.at[1])
        send(block(3, 0), block(3, 0), ss.at[0], rs.at[0], forward)
        arrive(block(1), rs.at[3])
        send(block(1, 1), block(1, 1), ss.at[2], rs.at[2], back)

    def finish(block, rs):
        arrive(block(2, 0), rs.at[0])
        arrive(block(2, 1), rs.at[2])

    y_next, y_last = device(x, turn(y, 1), z, k), device(x, turn(y, 3), z, k)
    z_next, z_last = device(x, y, turn(z, 1), k), device(x, y, turn(z, 3), k)

    def on_y(step, s, l):
        step(functools.partial(passages, s, l), p_s.at[s, l], p_r.at[s, l], y_next, y_last)

    def on_z(step, s, c):
        step(functools.partial(queries, s, c), q_s.at[s, c], q_r.at[s, c], z_next, z_last)

    for d in (1, 2, 3):
        send(idx.at[:, rows(z)], idx.at[:, rows(z)], i_s.at[d], i_r.at[z], device(x, y, turn(z, d), k))
    mine = pt.at[xh, half(xl, y)]
    send(p_buf.at[rows(xh, H)], mine, px_s.at[0], px_r.at[xh, xl], device(2 * xh + yon, y, z, k))
    send(p_buf.at[rows(far, H)], mine, px_s.at[1], px_r.at[xh, xl], device(2 * far + yon, y, z, k))
    on_y(spread, xh, xl)
    for n in range(2):
        on_z(spread, xh, n)
    for n in range(2):
        send(queries(xh, n, 0), queries(xh, n, 0), qf_s.at[n], qf_r.at[n], device(opposite, y, z, k))
    send(p_buf.at[rows(far, H)], mine, px_s.at[2], px_r.at[xh, xl], device(opposite, y, z, k))
    for s in range(2):
        send(table_part(s, 1 - k), pt.at[s, table_rows], t_s.at[0, s], t_s.at[1, s], sibling)
    for s in (xh, far):
        arrive(passages(s, yon, 0), px_r.at[s, yon])
        on_y(spread, s, yon)
    on_y(relay, xh, xl)
    on_z(relay, xh, 0)
    for d in (1, 2, 3):
        arrive(idx.at[:, rows(turn(z, d))], i_r.at[turn(z, d)])

    first = xh * 512 + z * TR
    place = lax.broadcasted_iota(jnp.int32, (2 * TR, NB * R), 0)
    named = (place + first + jnp.where(place >= TR, 256 - TR, 0)).astype(F32)
    count = jnp.zeros((2 * TR, NB * R), F32)
    for n in range(7):
        count += (idx[n:n + 1, :] == named).astype(F32)
    counts[...] = count
    on_z(relay, xh, 1)
    arrive(queries(far, 0, 0), qf_r.at[0])
    on_z(spread, far, 0)
    on_y(relay, xh, yon)
    arrive(queries(far, 1, 0), qf_r.at[1])
    on_z(spread, far, 1)
    on_y(relay, far, yon)
    arrive(passages(far, xl, 0), px_r.at[far, xl])
    on_y(spread, far, xl)

    other_rows = pl.ds(NB * R + pl.multiple_of((1 - k) * TR, TR), TR)
    for s in range(2):
        arrive(pt.at[s, other_rows], t_s.at[1, s])
        own_table[s].wait()
    nt = (((1,), (1,)), ((), ()))

    def logits_part(s, i):
        return lax.dot_general(pt[s, i * R:(i + 1) * R], qb[s], nt, preferred_element_type=F32)

    for n in range(2):
        finish(functools.partial(queries, xh, n), q_r.at[xh, n])
    for l in (xl, yon):
        finish(functools.partial(passages, xh, l), p_r.at[xh, l])
    for i in range(2):
        s_own[i * R:(i + 1) * R] = logits_part(xh, i)
    on_z(relay, far, 0)
    on_y(relay, far, xl)
    on_z(relay, far, 1)
    for i in range(2, COLS // R):
        s_own[i * R:(i + 1) * R] = logits_part(xh, i)
    for n in range(2):
        finish(functools.partial(queries, far, n), q_r.at[far, n])
    for l in (yon, xl):
        finish(functools.partial(passages, far, l), p_r.at[far, l])
    for i in range(COLS // R):
        s_own[i * R:(i + 1) * R] += logits_part(far, i)
        send(s_own.at[pl.ds(i * R, R)], s_far.at[pl.ds(i * R, R)], c_s.at[i], c_r.at[i], sibling)
    hit = jnp.zeros((1, NB * R), F32)
    positive = idx[7:8, :]

    def here(i):
        r = lax.broadcasted_iota(jnp.int32, (R, NB * R), 0)
        r = r + jnp.where(r >= H, 4 * R - H, 0) + (i // 2 * 2048 + i % 2 * 1024) + z * R + xh * H
        return r.astype(F32) == positive

    tops, masses = [], []
    count = counts[...]
    for i in range(COLS // R):
        arrive(s_far.at[pl.ds(i * R, R)], c_r.at[i])
        total = (s_own[i * R:(i + 1) * R] + s_far[i * R:(i + 1) * R]) * factor
        if i < NB:
            hit += jnp.sum(jnp.where(here(i), total, 0.0), axis=0, keepdims=True)
            top = jnp.max(total, axis=0, keepdims=True)
            e = jnp.exp(total - top)
        else:
            top = jnp.max(jnp.where(count > 0, total, -jnp.inf), axis=0, keepdims=True)
            e = count * jnp.exp(jnp.where(count > 0, total - top, 0.0))
        e_buf[i * R:(i + 1) * R] = e
        tops.append(top)
        masses.append(jnp.sum(e, axis=0, keepdims=True))
    top = functools.reduce(jnp.maximum, tops)
    mass = sum(m * jnp.exp(t - top) for m, t in zip(masses, tops))
    me = xh * 4 + z
    for n in range(NB):
        stats[me, n:n + 1] = top[:, n * R:(n + 1) * R]
        stats[me, NB + n:NB + n + 1] = mass[:, n * R:(n + 1) * R]
        hits[me, n:n + 1] = hit[:, n * R:(n + 1) * R]
    there = []
    for n in range(7, 0, -1):
        dx, d = n // 4, n % 4
        there.append(device(turn(x, 2 * dx), y, turn(z, d), k))
        send(stats.at[me], stats.at[me], st_s.at[0, n], st_r.at[0, me], there[-1])
    for n in range(7, 0, -1):
        send(hits.at[me], hits.at[me], st_s.at[1, n], st_r.at[1, me], there[7 - n])
    for n in range(1, 8):
        dx, d = n // 4, n % 4
        slot = lax.rem(xh + dx, 2) * 4 + turn(z, d)
        arrive(stats.at[slot], st_r.at[0, slot])
    row_top = stats[0, 0:NB]
    for n in range(1, 8):
        row_top = jnp.maximum(row_top, stats[n, 0:NB])
    mass = jnp.zeros((NB, R), F32)
    for n in range(8):
        mass += stats[n, NB:2 * NB] * jnp.exp(stats[n, 0:NB] - row_top)
    sums[...] = row_top + jnp.log(mass)
    log_total = jnp.concatenate([sums[n:n + 1] for n in range(NB)], axis=1)
    weight = idx[8:9, :] * factor
    for i in range(COLS // R):
        g = weight * jnp.exp(tops[i] - log_total) * e_buf[i * R:(i + 1) * R]
        if i < NB:
            g = g - jnp.where(here(i), weight, 0.0)
        grad[i * R:(i + 1) * R] = g.astype(BF16)

    nn, tn = (((1,), (0,)), ((), ())), (((0,), (0,)), ((), ()))

    def query_part(s, zz):
        return lax.dot_general(grad[:, rows(zz)], pt[s], tn, preferred_element_type=F32)

    def query_ahead(n, s):
        qg_part[n] = query_part(s, turn(z, 2)).astype(BF16)
        send(qg_part.at[n, pl.ds(0, H)], rqa.at[n, 0], qg_s.at[n, 0], qg_r.at[n, 0], z_next)
        send(qg_part.at[n, pl.ds(H, H)], rqa.at[n, 1], qg_s.at[n, 1], qg_r.at[n, 1], z_last)

    def query_next(n, s):
        for way, (d, to) in enumerate(((1, z_next), (3, z_last))):
            part = query_part(s, turn(z, d))
            arrive(rqa.at[n, way], qg_r.at[n, way])
            a, o = way * H, (1 - way) * H
            qg_on[n, way, a:a + H] = (part[a:a + H] + rqa[n, way].astype(F32)).astype(BF16)
            qg_on[n, way, o:o + H] = part[o:o + H].astype(BF16)
            send(qg_on.at[n, way], rq.at[n, way], qg_s.at[n, 2 + way], qg_r.at[n, 2 + way], to)

    def query_sum(n, total):
        for way in range(2):
            arrive(rq.at[n, way], qg_r.at[n, 2 + way])
            total += rq[n, way].astype(F32)
        return total

    Q = H // 2

    def passage_ahead(n):
        s, l = order[n]
        px[n] = lax.dot_general(grad[rows(l, 4 * H)], qb[s], nn, preferred_element_type=F32)
        pg_part[n] = px[n, rows(turn(y, 2), H)].astype(BF16)
        send(pg_part.at[n, pl.ds(0, Q)], rpa.at[n, 0], pg_s.at[n, 0], pg_r.at[n, 0], y_next)
        send(pg_part.at[n, pl.ds(Q, Q)], rpa.at[n, 1], pg_s.at[n, 1], pg_r.at[n, 1], y_last)

    def passage_next(n):
        for way, (d, to) in enumerate(((1, y_next), (3, y_last))):
            part = px[n, rows(turn(y, d), H)]
            arrive(rpa.at[n, way], pg_r.at[n, way])
            a, o = way * Q, (1 - way) * Q
            pg_on[n, way, a:a + Q] = (part[a:a + Q] + rpa[n, way].astype(F32)).astype(BF16)
            pg_on[n, way, o:o + Q] = part[o:o + Q].astype(BF16)
            send(pg_on.at[n, way], rp.at[n, way], pg_s.at[n, 2 + way], pg_r.at[n, 2 + way], to)

    def passage_sum(n):
        total = px[n, rows(y, H)]
        for way in range(2):
            arrive(rp.at[n, way], pg_r.at[n, 2 + way])
            total += rp[n, way].astype(F32)
        return total

    def passage_on(n):
        s, l = order[n]
        pg_sum[n] = passage_sum(n).astype(BF16)
        send(pg_sum.at[n], rpx.at[xh, xl], sx_s.at[n], sx_r.at[xh, xl], device(2 * s + l, y, z, k))

    def table_half(l):
        return lax.dot_general(grad[NB * R:], qb[l], nn, preferred_element_type=F32)

    order = ((far, xl), (far, yon), (xh, yon), (xh, xl))
    passage_ahead(0)
    query_ahead(0, far)
    tg_part[0] = table_half(yon).astype(BF16)
    send(tg_part.at[0], rtx, tx_s.at[0], tx_s.at[1], device(2 * xh + yon, y, z, k))
    passage_ahead(1)
    passage_ahead(2)
    query_ahead(1, xh)
    passage_ahead(3)
    tx[...] = table_half(xl)
    passage_next(0)
    query_next(0, far)
    passage_next(1)
    passage_next(2)

    arrive(rtx, tx_s.at[1])
    tx[...] += rtx[...].astype(F32)
    tg_part[1] = tx[...].astype(BF16)
    for d in (1, 2, 3):
        yy = turn(y, d)
        send(tg_part.at[1, :, rows(yy, CW)], rt.at[4 - d], tg_s.at[d], tg_r.at[4 - d], device(x, yy, z, k))

    query_next(1, xh)
    passage_next(3)
    qx[...] = query_part(far, z)
    passage_on(0)
    qg_sum[...] = query_sum(0, qx[...]).astype(BF16)
    send(qg_sum, rqx, qx_s.at[0], qx_s.at[1], device(opposite, y, z, k))
    passage_on(1)
    qg_out[...] = query_part(xh, z)

    total = tx[:, rows(y, CW)]
    for d in (1, 2, 3):
        arrive(rt.at[d], tg_r.at[d])
        total += rt[d].astype(F32)
    dst_y = 2 * k + lax.div(y, 2)
    for core in range(2):
        for h in range(2):
            tsum[core, h] = total[core * TR:(core + 1) * TR, h * 128:(h + 1) * 128]
            dst_z = 2 * lax.rem(y, 2) + h
            mine = (dst_y == y) & (dst_z == z) & (k == core)

            @pl.when(mine)
            def _():
                tt[z] = tsum[core, h]

            @pl.when(jnp.logical_not(mine))
            def _():
                send(tsum.at[core, h], tt.at[z], tt_s.at[core, h], tt_r.at[z], device(x, dst_y, dst_z, core))
                sends.pop()

    passage_on(2)
    total = query_sum(1, qg_out[...])
    arrive(rqx, qx_s.at[1])
    qg_out[...] = total + rqx[...].astype(F32)
    total = passage_sum(3)
    arrive(rpx.at[xh, yon], sx_r.at[xh, yon])
    pg_out[rows(xh, H)] = total + rpx[xh, yon].astype(F32)
    for l in range(2):
        arrive(rpx.at[far, l], sx_r.at[far, l])
    pg_out[rows(far, H)] = rpx[far, 0].astype(F32) + rpx[far, 1].astype(F32)
    src_y = 2 * lax.rem(y, 2) + lax.div(z, 2)
    src_k = lax.div(y, 2)
    for zz in range(4):
        @pl.when(jnp.logical_not((src_y == y) & (src_k == k) & (z == zz)))
        def _():
            arrive(tt.at[zz], tt_r.at[zz])

        tg_out[zz * TR:(zz + 1) * TR] = tt[zz]

    for n in range(1, 8):
        dx, d = n // 4, n % 4
        slot = lax.rem(xh + dx, 2) * 4 + turn(z, d)
        arrive(hits.at[slot], st_r.at[1, slot])
    hit = jnp.zeros((NB, R), F32)
    for n in range(8):
        hit += hits[n, 0:NB]
    own_block = lax.broadcasted_iota(jnp.int32, (NB, R), 0) == z
    own_loss = jnp.sum(jnp.where(own_block, sums[...] - hit, 0.0), axis=0, keepdims=True)
    loss_out[...] = pltpu.roll(jnp.broadcast_to(own_loss, (8, R)), lax.rem(R - c * 32, R), 1)

    for copy in sends:
        copy.wait_send()
    for core in range(2):
        for h in range(2):
            mine = (dst_y == y) & (2 * lax.rem(y, 2) + h == z) & (k == core)

            @pl.when(jnp.logical_not(mine))
            def _():
                src, sem = tsum.at[core, h], tt_s.at[core, h]
                pltpu.make_async_remote_copy(
                    src_ref=src, dst_ref=src, send_sem=sem, recv_sem=sem, device_id=sibling, device_id_type=MESH
                ).wait_send()


def place(loss_in, qg_in, pg_in, tg_in, loss_out, qg_out, pg_out, tg_out, sem):
    copies = []
    for n, (src, dst) in enumerate(((qg_in, qg_out), (pg_in, pg_out), (tg_in, tg_out))):
        copies.append(pltpu.make_async_copy(src, dst, sem.at[n]))
        copies[-1].start()
    loss_out[...] = loss_in[0:1, 0:32]
    for copy in copies:
        copy.wait()


def per_device(queries, passages, table, neg_owner, neg_row, positive, loss_weight):
    factor = float(queries.shape[1] * 4) ** (-0.5)
    vmem = pl.BlockSpec(memory_space=pltpu.VMEM)
    dma = pltpu.SemaphoreType.DMA
    loss, qg, pg, tg = pl.pallas_call(
        functools.partial(kernel, factor),
        name="contrastive",
        out_shape=(
            pltpu.VMEM((8, R), F32),
            pltpu.VMEM((R, W), F32),
            pltpu.VMEM((R, W), F32),
            pltpu.VMEM((4 * TR, 128), F32),
        ),
        in_specs=[pl.BlockSpec(memory_space=pl.ANY)] * 7,
        out_specs=[vmem] * 4,
        scratch_shapes=[
            pltpu.VMEM((2, NB * R, W), BF16),
            pltpu.VMEM((2, COLS, W), BF16),
            pltpu.VMEM((16, NB * R), F32),
            pltpu.VMEM((COLS, NB * R), F32),
            pltpu.VMEM((COLS, NB * R), F32),
            pltpu.VMEM((COLS, NB * R), F32),
            pltpu.VMEM((COLS, NB * R), BF16),
            pltpu.VMEM((8, 2 * NB, R), F32),
            pltpu.VMEM((8, 2 * NB, R), F32),
            pltpu.VMEM((2 * TR, NB * R), F32),
            pltpu.VMEM((2, R, W), BF16),
            pltpu.VMEM((4, H, W), BF16),
            pltpu.VMEM((2, 2 * TR, W), BF16),
            pltpu.VMEM((2, 2, R, W), BF16),
            pltpu.VMEM((4, 2, H, W), BF16),
            pltpu.VMEM((2, 2, H, W), BF16),
            pltpu.VMEM((4, 2, H // 2, W), BF16),
            pltpu.VMEM((R, W), BF16),
            pltpu.VMEM((3, H, W), BF16),
            pltpu.VMEM((2, 2, R, W), BF16),
            pltpu.VMEM((R, W), BF16),
            pltpu.VMEM((4, 2, H, W), BF16),
            pltpu.VMEM((2, 2, H, W), BF16),
            pltpu.VMEM((4, 2 * TR, CW), BF16),
            pltpu.VMEM((2 * TR, W), BF16),
            pltpu.VMEM((4, TR, 128), F32),
            pltpu.VMEM((R, W), F32),
            pltpu.VMEM((4, 4 * H, W), F32),
            pltpu.VMEM((2 * TR, W), F32),
            pltpu.VMEM((2, 2, TR, 128), F32),
            pltpu.VMEM((R, W), BF16),
            pltpu.VMEM((7, R), jnp.int32),
            pltpu.VMEM((7, R), jnp.int32),
            pltpu.VMEM((1, R), jnp.int32),
            pltpu.VMEM((1, R), F32),
            pltpu.VMEM((NB, R), F32),
            dma((8,)),
            dma((2, 2, 4)), dma((2, 2, 4)), dma((2,)), dma((2,)),
            dma((3,)), dma((2, 2)), dma((2, 2, 4)), dma((2, 2, 4)),
            dma((2, 2)),
            dma((4,)), dma((4,)),
            dma((5,)), dma((5,)),
            dma((2, 8)), dma((2, 8)),
            dma((2, 4)), dma((2, 4)),
            dma((2,)),
            dma((4, 4)), dma((4, 4)),
            dma((3,)), dma((2, 2)),
            dma((2,)), dma((4,)), dma((4,)),
            dma((2, 2)), dma((4,)),
        ],
        compiler_params=pltpu.CompilerParams(
            collective_id=0, has_side_effects=True, vmem_limit_bytes=48 * 2**20
        ),
    )(*[
        pltpu.with_memory_space_constraint(a, pltpu.HBM)
        for a in (queries, passages, table, neg_owner.T, neg_row.T, positive[None], loss_weight[None])
    ])
    loss, qg, pg, tg = pl.pallas_call(
        place,
        name="place",
        out_shape=(
            jax.ShapeDtypeStruct((1, 32), F32),
            jax.ShapeDtypeStruct((R, W), F32),
            jax.ShapeDtypeStruct((R, W), F32),
            jax.ShapeDtypeStruct((4 * TR, 128), F32),
        ),
        in_specs=[vmem] + [pl.BlockSpec(memory_space=pl.ANY)] * 3,
        out_specs=[vmem] + [pl.BlockSpec(memory_space=pl.ANY)] * 3,
        scratch_shapes=[dma((3,))],
    )(*[pltpu.with_memory_space_constraint(a, pltpu.VMEM) for a in (loss, qg, pg, tg)])
    return loss[0], qg, pg, tg


def solution(mesh):
    placed = (
        P("blk", "corpus"),
        P("blk", "corpus"),
        P("corpus", None),
        P("blk", None),
        P("blk", None),
        P("blk"),
        P("blk"),
    )
    return jax.shard_map(
        per_device,
        mesh=mesh,
        in_specs=placed,
        out_specs=(
            P(("blk", "corpus")),
            P("blk", "corpus"),
            P("blk", "corpus"),
            P("corpus", "blk"),
        ),
        check_vma=False,
    )
```

```python
import functools

import jax
import jax.numpy as jnp
from jax import lax
from jax.experimental import pallas as pl
from jax.experimental.pallas import tpu as pltpu
from jax.sharding import PartitionSpec as P

MESH = pl.DeviceIdType.MESH
F32 = jnp.float32
BF16 = jnp.bfloat16

R = 128
H = 64
W = 1024
NB = 4
TR = 64
COLS = NB * R + 2 * TR
CW = 256


def device(x, y, z, k):
    return (lax.rem(x, 2) * 16 + y * 4 + z, lax.div(x, 2) * 2 + k)


def kernel(
    factor, q_in, p_in, t_in, owner_in, row_in, pos_in, weight_in, loss_out, qg_out, pg_out, tg_out,
    qb, pt, idx, s_own, s_far, e_buf, grad, stats, hits, counts, qg_part, pg_part, tg_part,
    qg_on, pg_on, rqa, rpa, qg_sum, pg_sum, rq, rqx, rp, rpx, rt, rtx, tt, qx, qn, px, tx, tsum, p_buf, owner_buf, row_buf, pos_buf, weight_buf, sums,
    in_s, q_s, q_r, qf_s, qf_r, px_s, px_r, p_s, p_r, t_s, i_s, i_r, c_s, c_r, st_s, st_r,
    qg_s, qg_r, qx_s, qx_r, pg_s, pg_r, sx_s, sx_r, tx_s, tg_s, tg_r, tt_s, tt_r,
):
    b, c = lax.axis_index("blk"), lax.axis_index("corpus")
    xl, y, z = lax.div(b, 16), lax.rem(lax.div(b, 4), 4), lax.rem(b, 4)
    xh, k = lax.div(c, 2), lax.rem(c, 2)
    x = 2 * xh + xl
    far, yon = 1 - xh, 1 - xl
    opposite = 2 * far + xl
    sibling = device(x, y, z, 1 - k)

    def send(src, dst, ss, rs, where):
        copy = pltpu.make_async_remote_copy(
            src_ref=src, dst_ref=dst, send_sem=ss, recv_sem=rs, device_id=where, device_id_type=MESH
        )
        copy.start()
        sends.append(copy)

    def arrive(dst, rs):
        pltpu.make_async_remote_copy(
            src_ref=dst, dst_ref=dst, send_sem=rs, recv_sem=rs, device_id=sibling, device_id_type=MESH
        ).wait_recv()

    def stage(src, dst, sem):
        copy = pltpu.make_async_copy(src, dst, sem)
        copy.start()
        return copy

    def turn(v, d):
        return lax.rem(v + d, 4)

    def rows(i, n=R):
        return pl.ds(pl.multiple_of(i * n, n), n)

    def half(l, yy):
        return rows(l * 4 + yy, H)

    sends = []
    barrier = pltpu.get_barrier_semaphore()
    peers = [sibling]
    for d in (1, 2, 3):
        peers.append(device(turn(x, d), y, z, k))
        peers.append(device(x, turn(y, d), z, k))
        peers.append(device(x, y, turn(z, d), k))
    for peer in peers:
        pl.semaphore_signal(barrier, 1, device_id=peer, device_id_type=MESH)

    table_rows = pl.ds(NB * R + pl.multiple_of(k * TR, TR), TR)
    own = [
        stage(p_in, p_buf, in_s.at[0]),
        stage(q_in, qb.at[xh, rows(z)], in_s.at[1]),
        stage(owner_in, owner_buf, in_s.at[2]),
        stage(row_in, row_buf, in_s.at[3]),
        stage(pos_in, pos_buf, in_s.at[4]),
        stage(weight_in, weight_buf, in_s.at[5]),
    ]

    def table_part(s, core):
        return t_in.at[rows(z, TR), pl.ds(pl.multiple_of((2 * s + core) * W, W), W)]

    own_table = [stage(table_part(s, k), pt.at[s, table_rows], in_s.at[6 + s]) for s in range(2)]
    for copy in own:
        copy.wait()
    pt[xh, half(xl, y)] = p_buf[rows(xh, H)]
    idx[0:7, rows(z)] = (owner_buf[...] * 256 + row_buf[...]).astype(F32)
    idx[7:8, rows(z)] = pos_buf[...].astype(F32)
    idx[8:9, rows(z)] = weight_buf[...]
    pl.semaphore_wait(barrier, len(peers))

    def passages(s, l, d, part=None):
        return pt.at[s, half(l, turn(y, d)) if part is None else rows((l * 4 + turn(y, d)) * 2 + part, H // 2)]

    def queries(s, c, d, part=None):
        n = turn(z, d) * 2 + c
        return qb.at[s, rows(n, H) if part is None else rows(n * 2 + part, H // 2)]

    def spread(block, ss, rs, forward, back):
        send(block(0), block(0), ss.at[1], rs.at[1], forward)
        send(block(0), block(0), ss.at[3], rs.at[3], back)

    def relay(block, ss, rs, forward, back):
        arrive(block(3), rs.at[1])
        send(block(3, 0), block(3, 0), ss.at[0], rs.at[0], forward)
        arrive(block(1), rs.at[3])
        send(block(1, 1), block(1, 1), ss.at[2], rs.at[2], back)

    def finish(block, rs):
        arrive(block(2, 0), rs.at[0])
        arrive(block(2, 1), rs.at[2])

    y_next, y_last = device(x, turn(y, 1), z, k), device(x, turn(y, 3), z, k)
    z_next, z_last = device(x, y, turn(z, 1), k), device(x, y, turn(z, 3), k)

    def on_y(step, s, l):
        step(functools.partial(passages, s, l), p_s.at[s, l], p_r.at[s, l], y_next, y_last)

    def on_z(step, s, c):
        step(functools.partial(queries, s, c), q_s.at[s, c], q_r.at[s, c], z_next, z_last)

    for d in (1, 2, 3):
        send(idx.at[:, rows(z)], idx.at[:, rows(z)], i_s.at[d], i_r.at[z], device(x, y, turn(z, d), k))
    mine = pt.at[xh, half(xl, y)]
    send(p_buf.at[rows(xh, H)], mine, px_s.at[0], px_r.at[xh, xl], device(2 * xh + yon, y, z, k))
    send(p_buf.at[rows(far, H)], mine, px_s.at[1], px_r.at[xh, xl], device(2 * far + yon, y, z, k))
    on_y(spread, xh, xl)
    for n in range(2):
        on_z(spread, xh, n)
    for n in range(2):
        send(queries(xh, n, 0), queries(xh, n, 0), qf_s.at[n], qf_r.at[n], device(opposite, y, z, k))
    send(p_buf.at[rows(far, H)], mine, px_s.at[2], px_r.at[xh, xl], device(opposite, y, z, k))
    for s in range(2):
        send(table_part(s, 1 - k), pt.at[s, table_rows], t_s.at[0, s], t_s.at[1, s], sibling)
    for s in (xh, far):
        arrive(passages(s, yon, 0), px_r.at[s, yon])
        on_y(spread, s, yon)
    on_y(relay, xh, xl)
    on_z(relay, xh, 0)
    for d in (1, 2, 3):
        arrive(idx.at[:, rows(turn(z, d))], i_r.at[turn(z, d)])

    first = xh * 512 + z * TR
    place = lax.broadcasted_iota(jnp.int32, (2 * TR, NB * R), 0)
    named = (place + first + jnp.where(place >= TR, 256 - TR, 0)).astype(F32)
    count = jnp.zeros((2 * TR, NB * R), F32)
    for n in range(7):
        count += (idx[n:n + 1, :] == named).astype(F32)
    counts[...] = count
    on_z(relay, xh, 1)
    arrive(queries(far, 0, 0), qf_r.at[0])
    on_z(spread, far, 0)
    on_y(relay, xh, yon)
    arrive(queries(far, 1, 0), qf_r.at[1])
    on_z(spread, far, 1)
    on_y(relay, far, yon)
    arrive(passages(far, xl, 0), px_r.at[far, xl])
    on_y(spread, far, xl)

    other_rows = pl.ds(NB * R + pl.multiple_of((1 - k) * TR, TR), TR)
    for s in range(2):
        arrive(pt.at[s, other_rows], t_s.at[1, s])
        own_table[s].wait()
    nt = (((1,), (1,)), ((), ()))

    def logits_part(s, i):
        return lax.dot_general(pt[s, i * R:(i + 1) * R], qb[s], nt, preferred_element_type=F32)

    for n in range(2):
        finish(functools.partial(queries, xh, n), q_r.at[xh, n])
    for l in (xl, yon):
        finish(functools.partial(passages, xh, l), p_r.at[xh, l])
    for i in range(2):
        s_own[i * R:(i + 1) * R] = logits_part(xh, i)
    on_z(relay, far, 0)
    on_y(relay, far, xl)
    on_z(relay, far, 1)
    for i in range(2, COLS // R):
        s_own[i * R:(i + 1) * R] = logits_part(xh, i)
    for n in range(2):
        finish(functools.partial(queries, far, n), q_r.at[far, n])
    for l in (yon, xl):
        finish(functools.partial(passages, far, l), p_r.at[far, l])
    for i in range(COLS // R):
        s_own[i * R:(i + 1) * R] += logits_part(far, i)
        send(s_own.at[pl.ds(i * R, R)], s_far.at[pl.ds(i * R, R)], c_s.at[i], c_r.at[i], sibling)
    hit = jnp.zeros((1, NB * R), F32)
    positive = idx[7:8, :]

    def here(i):
        r = lax.broadcasted_iota(jnp.int32, (R, NB * R), 0)
        r = r + jnp.where(r >= H, 4 * R - H, 0) + (i // 2 * 2048 + i % 2 * 1024) + z * R + xh * H
        return r.astype(F32) == positive

    tops, masses = [], []
    count = counts[...]
    for i in range(COLS // R):
        arrive(s_far.at[pl.ds(i * R, R)], c_r.at[i])
        total = (s_own[i * R:(i + 1) * R] + s_far[i * R:(i + 1) * R]) * factor
        if i < NB:
            hit += jnp.sum(jnp.where(here(i), total, 0.0), axis=0, keepdims=True)
            top = jnp.max(total, axis=0, keepdims=True)
            e = jnp.exp(total - top)
        else:
            top = jnp.max(jnp.where(count > 0, total, -jnp.inf), axis=0, keepdims=True)
            e = count * jnp.exp(jnp.where(count > 0, total - top, 0.0))
        e_buf[i * R:(i + 1) * R] = e
        tops.append(top)
        masses.append(jnp.sum(e, axis=0, keepdims=True))
    top = functools.reduce(jnp.maximum, tops)
    mass = sum(m * jnp.exp(t - top) for m, t in zip(masses, tops))
    me = xh * 4 + z
    for n in range(NB):
        stats[me, n:n + 1] = top[:, n * R:(n + 1) * R]
        stats[me, NB + n:NB + n + 1] = mass[:, n * R:(n + 1) * R]
        hits[me, n:n + 1] = hit[:, n * R:(n + 1) * R]
    there = []
    for n in range(7, 0, -1):
        dx, d = n // 4, n % 4
        there.append(device(turn(x, 2 * dx), y, turn(z, d), k))
        send(stats.at[me], stats.at[me], st_s.at[0, n], st_r.at[0, me], there[-1])
    for n in range(7, 0, -1):
        send(hits.at[me], hits.at[me], st_s.at[1, n], st_r.at[1, me], there[7 - n])
    for n in range(1, 8):
        dx, d = n // 4, n % 4
        slot = lax.rem(xh + dx, 2) * 4 + turn(z, d)
        arrive(stats.at[slot], st_r.at[0, slot])
    row_top = stats[0, 0:NB]
    for n in range(1, 8):
        row_top = jnp.maximum(row_top, stats[n, 0:NB])
    mass = jnp.zeros((NB, R), F32)
    for n in range(8):
        mass += stats[n, NB:2 * NB] * jnp.exp(stats[n, 0:NB] - row_top)
    sums[...] = row_top + jnp.log(mass)
    log_total = jnp.concatenate([sums[n:n + 1] for n in range(NB)], axis=1)
    weight = idx[8:9, :] * factor
    for i in range(COLS // R):
        g = weight * jnp.exp(tops[i] - log_total) * e_buf[i * R:(i + 1) * R]
        if i < NB:
            g = g - jnp.where(here(i), weight, 0.0)
        grad[i * R:(i + 1) * R] = g.astype(BF16)

    nn, tn = (((1,), (0,)), ((), ())), (((0,), (0,)), ((), ()))

    def query_part(s, zz):
        return lax.dot_general(grad[:, rows(zz)], pt[s], tn, preferred_element_type=F32)

    def query_ahead(n, s):
        qg_part[n] = query_part(s, turn(z, 2)).astype(BF16)
        send(qg_part.at[n, pl.ds(0, H)], rqa.at[n, 0], qg_s.at[n, 0], qg_r.at[n, 0], z_next)
        send(qg_part.at[n, pl.ds(H, H)], rqa.at[n, 1], qg_s.at[n, 1], qg_r.at[n, 1], z_last)

    def query_next(n, s):
        ways = ((1, z_next), (3, z_last))
        for way, (d, to) in enumerate(ways):
            qn[way] = query_part(s, turn(z, d))
        for chunk in range(2):
            at = pl.ds(chunk * H, H)
            for way, (d, to) in enumerate(ways):
                part = qn[way, chunk * H:(chunk + 1) * H]
                if chunk == way:
                    arrive(rqa.at[n, way], qg_r.at[n, way])
                    part += rqa[n, way].astype(F32)
                qg_on[n, way, chunk * H:(chunk + 1) * H] = part.astype(BF16)
                sem = 2 + chunk * 2 + way
                send(qg_on.at[n, way, at], rq.at[n, way, at], qg_s.at[n, sem], qg_r.at[n, sem], to)

    def query_sum(n, chunk, total):
        for way in range(2):
            arrive(rq.at[n, way, pl.ds(chunk * H, H)], qg_r.at[n, 2 + chunk * 2 + way])
            total += rq[n, way, chunk * H:(chunk + 1) * H].astype(F32)
        return total

    def query_on(chunk):
        at = pl.ds(chunk * H, H)
        qg_sum[chunk * H:(chunk + 1) * H] = query_sum(0, chunk, qx[chunk * H:(chunk + 1) * H]).astype(BF16)
        send(qg_sum.at[at], rqx.at[at], qx_s.at[chunk], qx_r.at[chunk], device(opposite, y, z, k))

    Q = H // 2

    def passage_ahead(n):
        s, l = order[n]
        px[n] = lax.dot_general(grad[rows(l, 4 * H)], qb[s], nn, preferred_element_type=F32)
        pg_part[n] = px[n, rows(turn(y, 2), H)].astype(BF16)
        send(pg_part.at[n, pl.ds(0, Q)], rpa.at[n, 0], pg_s.at[n, 0], pg_r.at[n, 0], y_next)
        send(pg_part.at[n, pl.ds(Q, Q)], rpa.at[n, 1], pg_s.at[n, 1], pg_r.at[n, 1], y_last)

    def passage_next(n):
        for way, (d, to) in enumerate(((1, y_next), (3, y_last))):
            part = px[n, rows(turn(y, d), H)]
            arrive(rpa.at[n, way], pg_r.at[n, way])
            a, o = way * Q, (1 - way) * Q
            pg_on[n, way, a:a + Q] = (part[a:a + Q] + rpa[n, way].astype(F32)).astype(BF16)
            pg_on[n, way, o:o + Q] = part[o:o + Q].astype(BF16)
            send(pg_on.at[n, way], rp.at[n, way], pg_s.at[n, 2 + way], pg_r.at[n, 2 + way], to)

    def passage_sum(n):
        total = px[n, rows(y, H)]
        for way in range(2):
            arrive(rp.at[n, way], pg_r.at[n, 2 + way])
            total += rp[n, way].astype(F32)
        return total

    def passage_on(n):
        s, l = order[n]
        pg_sum[n] = passage_sum(n).astype(BF16)
        send(pg_sum.at[n], rpx.at[xh, xl], sx_s.at[n], sx_r.at[xh, xl], device(2 * s + l, y, z, k))

    def table_half(l):
        return lax.dot_general(grad[NB * R:], qb[l], nn, preferred_element_type=F32)

    order = ((far, xl), (far, yon), (xh, yon), (xh, xl))
    passage_ahead(0)
    query_ahead(0, far)
    tg_part[0] = table_half(yon).astype(BF16)
    send(tg_part.at[0], rtx, tx_s.at[0], tx_s.at[1], device(2 * xh + yon, y, z, k))
    passage_ahead(1)
    passage_ahead(2)
    query_ahead(1, xh)
    passage_ahead(3)
    tx[...] = table_half(xl)
    passage_next(0)
    query_next(0, far)
    passage_next(1)
    passage_next(2)

    arrive(rtx, tx_s.at[1])
    tx[...] += rtx[...].astype(F32)
    tg_part[1] = tx[...].astype(BF16)
    for d in (1, 2, 3):
        yy = turn(y, d)
        send(tg_part.at[1, :, rows(yy, CW)], rt.at[4 - d], tg_s.at[d], tg_r.at[4 - d], device(x, yy, z, k))

    query_next(1, xh)
    passage_next(3)
    qx[...] = query_part(far, z)
    passage_on(0)
    query_on(0)
    passage_on(1)
    query_on(1)
    qg_out[...] = query_part(xh, z)
    passage_on(2)

    total = tx[:, rows(y, CW)]
    for d in (1, 2, 3):
        arrive(rt.at[d], tg_r.at[d])
        total += rt[d].astype(F32)
    dst_y = 2 * k + lax.div(y, 2)
    for core in range(2):
        for h in range(2):
            tsum[core, h] = total[core * TR:(core + 1) * TR, h * 128:(h + 1) * 128]
            dst_z = 2 * lax.rem(y, 2) + h
            mine = (dst_y == y) & (dst_z == z) & (k == core)

            @pl.when(mine)
            def _():
                tt[z] = tsum[core, h]

            @pl.when(jnp.logical_not(mine))
            def _():
                send(tsum.at[core, h], tt.at[z], tt_s.at[core, h], tt_r.at[z], device(x, dst_y, dst_z, core))
                sends.pop()

    for chunk in range(2):
        at = slice(chunk * H, (chunk + 1) * H)
        total = query_sum(1, chunk, qg_out[at])
        arrive(rqx.at[pl.ds(chunk * H, H)], qx_r.at[chunk])
        qg_out[at] = total + rqx[at].astype(F32)
    total = passage_sum(3)
    arrive(rpx.at[xh, yon], sx_r.at[xh, yon])
    pg_out[rows(xh, H)] = total + rpx[xh, yon].astype(F32)
    for l in range(2):
        arrive(rpx.at[far, l], sx_r.at[far, l])
    pg_out[rows(far, H)] = rpx[far, 0].astype(F32) + rpx[far, 1].astype(F32)
    src_y = 2 * lax.rem(y, 2) + lax.div(z, 2)
    src_k = lax.div(y, 2)
    for zz in range(4):
        @pl.when(jnp.logical_not((src_y == y) & (src_k == k) & (z == zz)))
        def _():
            arrive(tt.at[zz], tt_r.at[zz])

        tg_out[zz * TR:(zz + 1) * TR] = tt[zz]

    for n in range(1, 8):
        dx, d = n // 4, n % 4
        slot = lax.rem(xh + dx, 2) * 4 + turn(z, d)
        arrive(hits.at[slot], st_r.at[1, slot])
    hit = jnp.zeros((NB, R), F32)
    for n in range(8):
        hit += hits[n, 0:NB]
    own_block = lax.broadcasted_iota(jnp.int32, (NB, R), 0) == z
    own_loss = jnp.sum(jnp.where(own_block, sums[...] - hit, 0.0), axis=0, keepdims=True)
    loss_out[...] = pltpu.roll(jnp.broadcast_to(own_loss, (8, R)), lax.rem(R - c * 32, R), 1)

    for copy in sends:
        copy.wait_send()
    for core in range(2):
        for h in range(2):
            mine = (dst_y == y) & (2 * lax.rem(y, 2) + h == z) & (k == core)

            @pl.when(jnp.logical_not(mine))
            def _():
                src, sem = tsum.at[core, h], tt_s.at[core, h]
                pltpu.make_async_remote_copy(
                    src_ref=src, dst_ref=src, send_sem=sem, recv_sem=sem, device_id=sibling, device_id_type=MESH
                ).wait_send()


def place(loss_in, qg_in, pg_in, tg_in, loss_out, qg_out, pg_out, tg_out, sem):
    copies = []
    for n, (src, dst) in enumerate(((qg_in, qg_out), (pg_in, pg_out), (tg_in, tg_out))):
        copies.append(pltpu.make_async_copy(src, dst, sem.at[n]))
        copies[-1].start()
    loss_out[...] = loss_in[0:1, 0:32]
    for copy in copies:
        copy.wait()


def per_device(queries, passages, table, neg_owner, neg_row, positive, loss_weight):
    factor = float(queries.shape[1] * 4) ** (-0.5)
    vmem = pl.BlockSpec(memory_space=pltpu.VMEM)
    dma = pltpu.SemaphoreType.DMA
    loss, qg, pg, tg = pl.pallas_call(
        functools.partial(kernel, factor),
        name="contrastive",
        out_shape=(
            pltpu.VMEM((8, R), F32),
            pltpu.VMEM((R, W), F32),
            pltpu.VMEM((R, W), F32),
            pltpu.VMEM((4 * TR, 128), F32),
        ),
        in_specs=[pl.BlockSpec(memory_space=pl.ANY)] * 7,
        out_specs=[vmem] * 4,
        scratch_shapes=[
            pltpu.VMEM((2, NB * R, W), BF16),
            pltpu.VMEM((2, COLS, W), BF16),
            pltpu.VMEM((16, NB * R), F32),
            pltpu.VMEM((COLS, NB * R), F32),
            pltpu.VMEM((COLS, NB * R), F32),
            pltpu.VMEM((COLS, NB * R), F32),
            pltpu.VMEM((COLS, NB * R), BF16),
            pltpu.VMEM((8, 2 * NB, R), F32),
            pltpu.VMEM((8, 2 * NB, R), F32),
            pltpu.VMEM((2 * TR, NB * R), F32),
            pltpu.VMEM((2, R, W), BF16),
            pltpu.VMEM((4, H, W), BF16),
            pltpu.VMEM((2, 2 * TR, W), BF16),
            pltpu.VMEM((2, 2, R, W), BF16),
            pltpu.VMEM((4, 2, H, W), BF16),
            pltpu.VMEM((2, 2, H, W), BF16),
            pltpu.VMEM((4, 2, H // 2, W), BF16),
            pltpu.VMEM((R, W), BF16),
            pltpu.VMEM((3, H, W), BF16),
            pltpu.VMEM((2, 2, R, W), BF16),
            pltpu.VMEM((R, W), BF16),
            pltpu.VMEM((4, 2, H, W), BF16),
            pltpu.VMEM((2, 2, H, W), BF16),
            pltpu.VMEM((4, 2 * TR, CW), BF16),
            pltpu.VMEM((2 * TR, W), BF16),
            pltpu.VMEM((4, TR, 128), F32),
            pltpu.VMEM((R, W), F32),
            pltpu.VMEM((2, R, W), F32),
            pltpu.VMEM((4, 4 * H, W), F32),
            pltpu.VMEM((2 * TR, W), F32),
            pltpu.VMEM((2, 2, TR, 128), F32),
            pltpu.VMEM((R, W), BF16),
            pltpu.VMEM((7, R), jnp.int32),
            pltpu.VMEM((7, R), jnp.int32),
            pltpu.VMEM((1, R), jnp.int32),
            pltpu.VMEM((1, R), F32),
            pltpu.VMEM((NB, R), F32),
            dma((8,)),
            dma((2, 2, 4)), dma((2, 2, 4)), dma((2,)), dma((2,)),
            dma((3,)), dma((2, 2)), dma((2, 2, 4)), dma((2, 2, 4)),
            dma((2, 2)),
            dma((4,)), dma((4,)),
            dma((5,)), dma((5,)),
            dma((2, 8)), dma((2, 8)),
            dma((2, 6)), dma((2, 6)),
            dma((2,)), dma((2,)),
            dma((4, 4)), dma((4, 4)),
            dma((3,)), dma((2, 2)),
            dma((2,)), dma((4,)), dma((4,)),
            dma((2, 2)), dma((4,)),
        ],
        compiler_params=pltpu.CompilerParams(
            collective_id=0, has_side_effects=True, vmem_limit_bytes=48 * 2**20
        ),
    )(*[
        pltpu.with_memory_space_constraint(a, pltpu.HBM)
        for a in (queries, passages, table, neg_owner.T, neg_row.T, positive[None], loss_weight[None])
    ])
    loss, qg, pg, tg = pl.pallas_call(
        place,
        name="place",
        out_shape=(
            jax.ShapeDtypeStruct((1, 32), F32),
            jax.ShapeDtypeStruct((R, W), F32),
            jax.ShapeDtypeStruct((R, W), F32),
            jax.ShapeDtypeStruct((4 * TR, 128), F32),
        ),
        in_specs=[vmem] + [pl.BlockSpec(memory_space=pl.ANY)] * 3,
        out_specs=[vmem] + [pl.BlockSpec(memory_space=pl.ANY)] * 3,
        scratch_shapes=[dma((3,))],
    )(*[pltpu.with_memory_space_constraint(a, pltpu.VMEM) for a in (loss, qg, pg, tg)])
    return loss[0], qg, pg, tg


def solution(mesh):
    placed = (
        P("blk", "corpus"),
        P("blk", "corpus"),
        P("corpus", None),
        P("blk", None),
        P("blk", None),
        P("blk"),
        P("blk"),
    )
    return jax.shard_map(
        per_device,
        mesh=mesh,
        in_specs=placed,
        out_specs=(
            P(("blk", "corpus")),
            P("blk", "corpus"),
            P("blk", "corpus"),
            P("corpus", "blk"),
        ),
        check_vma=False,
    )
```
